128 devices in a mesh: seq: 16 (over z, y), col: 8 (over x, core).
Axes of the slice: x: 4, y: 4, z: 4, core: 2. Of those that a mesh axis runs over, the one named last changes fastest.
Arguments:
- item_table: bfloat16 [65536, 512], P('seq', 'col'), may hold values from -6 to 6
- hot_table: bfloat16 [256, 512], P(None, 'col'), may hold values from -6 to 6
- weight_in: bfloat16 [2, 512, 2048], replicated, may hold values from -0.25 to 0.25
- weight_out: bfloat16 [2, 512, 512], replicated, may hold values from -0.25 to 0.25
- row_owner: int32 [32768, 1], P('seq'), may hold values from 0 to 15; in each aligned block of 2048 rows (0 to 2047, 2048 to 4095, ...) at most 256 rows name the same one
- item_row: int32 [32768], P('seq'), may hold values from 0 to 4095
- hot_flag: int32 [32768], P('seq'), may hold values 0 or 1
- hot_row: int32 [32768], P('seq'), may hold values from 0 to 255
- segment: int32 [128, 256], P(('seq', 'col')), may hold values from 0 to 7, never falling along the last dimension, each value on 1 to 128 neighbouring positions
- cotangent: bfloat16 [32768, 512], P(('seq', 'col')), may hold values from -6 to 6
Outputs:
- encoded: bfloat16 [32768, 512], P(('seq', 'col'))
- table_grad: float32 [65536, 512], P('seq', 'col')
- hot_grad: float32 [256, 512], P(None, 'col')
- weight_in_grad: float32 [2, 512, 2048], replicated
- weight_out_grad: float32 [2, 512, 512], replicated
The draws below stay inside these ranges and needn't reach their ends.
Inputs may be any that keep to these rules, and one draw needn't show every extreme that they name: `row_owner`: in each aligned block of 256 * 8 positions (the positions of one index of seq) no owner is named by more than 256 positions, a bound that some block reaches. `segment`: segment numbers never fall along a block; each history holds 1 to 128 positions.
All inputs are finite; a program needn't handle non-finite values. No bound on the sum of `hot_flag` on one device may be relied on, other than what follows from the above.
Results may differ from the reference program's by a relative error of at most 0.028.
Values may be sent and summed in bfloat16 or wider, within the bound.
No kernel may reach another device: no remote copies, remote signals or barrier semaphores. Data moves between devices by JAX's collectives and lax.ppermute only.
A program may use at most 128 MiB of HBM per device.

```python
import math
import jax
import jax.numpy as jnp
import numpy as np
from jax import lax

D = 512
HEADS = 4
HEAD_DIM = 128
LAYERS = 2
TOK_DEV = 256
SEGS = 8
ITEMS_DEV = 4096
HOT = 256
CAP = 256
TOKENS = 32768
OWNERS = 128
ITEMS = 65536
N_SEQ = 16
N_COL = 8


def set_ends(array, stream_key, least, top_value):
    shape = array.shape
    index_at = [jax.random.randint(jax.random.fold_in(stream_key, axis), (), 0, shape[axis]) for axis in range(len(shape))]
    array = array.at[tuple(index_at)].set(least)
    longest = shape.index(max(shape))
    index_at[longest] = (index_at[longest] + 1) % shape[longest]
    return array.at[tuple(index_at)].set(top_value)


def block_scale(key, dims, cuts, low, largest):
    def one(axis_at, parts):
        heights = jax.random.uniform(jax.random.fold_in(jax.random.fold_in(key, 6), axis_at), (parts,), jnp.float32, low / len(cuts), largest / len(cuts))
        return jnp.repeat(jnp.exp(heights), dims[axis_at] // parts).reshape((-1,) + (1,) * (len(dims) - axis_at - 1))

    gain = one(*cuts[0])
    for cut in cuts[1:]:
        gain = gain * one(*cut)
    return gain


def length_profile(number_of, total, bound, slope):
    portions = [(1 << 20) // math.isqrt(standing ** slope) + 1 for standing in range(2, number_of + 1)]
    spare, given = total - bound - (number_of - 1), [1] * (number_of - 1)
    while spare > 0:
        candidates = [i for i in range(number_of - 1) if given[i] < bound]
        pool, budget = sum([portions[i] for i in candidates]), spare
        for i in candidates:
            more = min(bound - given[i], max(1, budget * portions[i] // pool), spare)
            given[i] = given[i] + more
            spare = spare - more
    return np.array([bound] + given)


def ragged_sizes(own_key, amount, total, most, skew):
    if amount == 2:
        one = jax.random.randint(own_key, (), max(1, total - most), min(most, total - 1) + 1)
        return jnp.stack([one, total - one])
    sizes = jnp.asarray(length_profile(amount, total, most, skew), jnp.int32)
    pairs = (amount - 1) // 2
    donor, receiver = sizes[1:1 + 2 * pairs:2], sizes[2:2 + 2 * pairs:2]
    slack = jnp.minimum(donor - 1, most - receiver)
    moved = jax.random.randint(jax.random.fold_in(own_key, 1), (pairs,), 0, 1 << 20) % (slack + 1)
    sizes = sizes.at[1:1 + 2 * pairs:2].set(donor - moved).at[2:2 + 2 * pairs:2].set(receiver + moved)
    return sizes[jax.random.permutation(jax.random.fold_in(own_key, 2), amount)]


def shared_out(key, own, number, rows, number_of, top, bound, lean):
    sequence = jax.random.permutation(key, number_of)
    packed, ordinary = load_shares(number_of, rows * top, bound, lean, True), load_shares(number_of, rows * top, bound, lean, False)
    places = jnp.arange(number_of)

    def named(lengths, turn):
        used = int((lengths > 0).sum())
        fixed = max(1, used // 4)
        passed = fixed + (places - fixed + turn * (used - fixed)) % max(1, number_of - fixed)
        return jnp.zeros((number_of,), jnp.int32).at[sequence[jnp.where(places < fixed, places, passed)]].set(jnp.asarray(lengths, jnp.int32))

    lengths = jnp.where(number % 4 == 0, named(packed, number // 4), named(ordinary, number - number // 4 - 1))
    mixed = jax.random.permutation(jax.random.fold_in(own, 3), number_of)
    source_of, sink = mixed[0:number_of // 2 * 2:2], mixed[1:number_of // 2 * 2:2]
    room = jnp.minimum(lengths[source_of] - 1, bound - lengths[sink]) // 2
    room = jnp.where((source_of == sequence[0]) | (sink == sequence[0]) | (lengths[sink] == 0), 0, jnp.maximum(room, 0))
    passed = jax.random.randint(jax.random.fold_in(own, 4), (number_of // 2,), 0, 1 << 20) % (room + 1)
    lengths = lengths.at[source_of].add(-passed).at[sink].add(passed)
    labels = jnp.searchsorted(jnp.cumsum(lengths), jnp.arange(rows * top), side="right").astype(jnp.int32)
    table = labels.reshape(top, rows).T
    table = table[jax.random.permutation(jax.random.fold_in(own, 1), rows)]
    turn = jax.random.randint(jax.random.fold_in(own, 2), (rows, 1), 0, top)
    return jnp.take_along_axis(table, (jnp.arange(top)[None, :] + turn) % top, axis=1)


def load_shares(count, total, reach, slope, full):
    loads = [(1 << 20) // math.isqrt(rank ** slope) + 1 for rank in range(1, count + 1)]
    largest = reach if full else min(reach, max(-(-total // count), total * loads[0] // sum(loads)))
    least = 1 if total - largest >= count - 1 else 0
    holding, surplus = [largest] + [least] * (count - 1), total - largest - least * (count - 1)
    while surplus > 0:
        candidates = [i for i in range(1, count) if holding[i] < largest] or [i for i in range(1, count) if holding[i] < reach]
        mass, remaining = sum([loads[i] for i in candidates]), surplus
        for i in candidates:
            more = min(reach - holding[i], max(1, remaining * loads[i] // mass), surplus)
            holding[i] = holding[i] + more
            surplus = surplus - more
    return np.array(holding)


def normal_values(key, extent, width, reach, cuts=(), dtype=jnp.bfloat16):
    drawn = width * jax.random.normal(key, extent, jnp.float32)
    if cuts:
        drawn = drawn * block_scale(key, extent, cuts, -0.22, 0.18)
    return jnp.clip(drawn, -reach, reach).astype(dtype)


def setup_inputs(seed: int = 0) -> dict:
    key_of = jax.random.split(jax.random.key(seed), 11)
    item_table = normal_values(key_of[0], (ITEMS, D), 1.0, 6.0, ((0, 16), (1, 8)))
    hot_table = normal_values(key_of[1], (HOT, D), 1.0, 6.0, ((1, 8),))
    weight_in = normal_values(key_of[2], (LAYERS, D, 4 * D), D ** -0.5, 0.25)
    weight_out = normal_values(key_of[3], (LAYERS, D, D), D ** -0.5, 0.25)
    row_owner_keys = jax.random.split(jax.random.fold_in(key_of[4], 1), TOKENS // (TOK_DEV * N_COL))
    row_owner_turns = jax.random.permutation(jax.random.fold_in(key_of[4], 3), TOKENS // (TOK_DEV * N_COL))
    row_owner = jax.vmap(lambda own, number: shared_out(jax.random.fold_in(key_of[4], 2), own, number, TOK_DEV * N_COL, N_SEQ, 1, CAP, 2))(row_owner_keys, row_owner_turns).reshape((TOKENS, 1))
    item_row = set_ends(jax.random.randint(key_of[5], (TOKENS,), 0, ITEMS_DEV), jax.random.fold_in(key_of[5], 1), 0, ITEMS_DEV - 1).astype(jnp.int32)
    hot_flag = set_ends((jax.random.randint(key_of[6], (TOKENS,), 0, 4) < 1).astype(jnp.int32), jax.random.fold_in(key_of[6], 1), 0, 1)
    hot_row = set_ends(jax.random.randint(key_of[7], (TOKENS,), 0, HOT), jax.random.fold_in(key_of[7], 1), 0, HOT - 1).astype(jnp.int32)
    segment = jax.vmap(lambda own: jnp.searchsorted(jnp.cumsum(ragged_sizes(own, SEGS, TOK_DEV, TOK_DEV // 2, 2)), jnp.arange(TOK_DEV), side="right"))(jax.random.split(key_of[8], OWNERS)).reshape((OWNERS, TOK_DEV)).astype(jnp.int32)
    cotangent = normal_values(key_of[9], (TOKENS, D), 1.0, 6.0, ((0, 128),))
    return {"item_table": item_table, "hot_table": hot_table, "weight_in": weight_in, "weight_out": weight_out, "row_owner": row_owner, "item_row": item_row, "hot_flag": hot_flag, "hot_row": hot_row, "segment": segment, "cotangent": cotangent}


def layer_norm(stream):
    center = stream - lax.optimization_barrier(jnp.mean(stream, axis=-1, keepdims=True))
    variance = lax.optimization_barrier(jnp.mean(center * center, axis=-1, keepdims=True))
    return center * lax.rsqrt(variance + 1e-05)

def causal_mask(segment_ids):
    position = jnp.arange(segment_ids.shape[0])
    return (segment_ids[:, None] == segment_ids[None, :]) & (position[None, :] <= position[:, None])

def hstu_layer(stream, proj_in, proj_out, allowed):
    count_rows = stream.shape[0]
    normed = layer_norm(stream).astype(jnp.bfloat16)
    projected = jax.nn.silu(jnp.dot(normed, proj_in, preferred_element_type=jnp.float32)).astype(jnp.bfloat16)
    gates, values, queries, key_part = jnp.split(projected, 4, axis=1)
    queries = queries.reshape(count_rows, HEADS, HEAD_DIM).astype(jnp.float32)
    key_part = key_part.reshape(count_rows, HEADS, HEAD_DIM).astype(jnp.float32)
    values = values.reshape(count_rows, HEADS, HEAD_DIM).astype(jnp.float32)
    scores = jnp.einsum('qhd,khd->hqk', queries, key_part) * HEAD_DIM ** (-0.5)
    attn = jnp.where(allowed[None], jax.nn.silu(scores), 0.0).astype(jnp.bfloat16)
    mixed = jnp.einsum('hqk,khd->qhd', attn.astype(jnp.float32), values).reshape(count_rows, D)
    gated = (layer_norm(mixed) * gates.astype(jnp.float32)).astype(jnp.bfloat16)
    return stream + jnp.dot(gated, proj_out, preferred_element_type=jnp.float32)

def run_stack(embedded, weight_in, weight_out, allowed):
    stream = embedded.astype(jnp.float32)
    for layer_index in range(LAYERS):
        stream = hstu_layer(stream, weight_in[layer_index], weight_out[layer_index], allowed)
    return stream.astype(jnp.bfloat16)

def reference(item_table, hot_table, weight_in, weight_out, row_owner, item_row, hot_flag, hot_row, segment, cotangent):
    regular = hot_flag == 0
    global_row = (row_owner[:, 0] * ITEMS_DEV + item_row).astype(jnp.int32)
    embedded = jnp.where(regular[:, None], item_table[global_row], hot_table[hot_row])
    block_rows = embedded.reshape(OWNERS, TOK_DEV, D)
    cot_blocks = cotangent.reshape(OWNERS, TOK_DEV, D)

    def per_block(totals, inputs):
        rows_here, segment_ids, block_cot = inputs
        allowed = causal_mask(segment_ids)

        def stack_here(emb_here, first, second):
            return run_stack(emb_here, first, second, allowed)
        encoded_here, pullback = jax.vjp(stack_here, rows_here, weight_in, weight_out)
        grad_emb, grad_first, grad_second = pullback(block_cot)
        totals = (totals[0] + grad_first.astype(jnp.float32), totals[1] + grad_second.astype(jnp.float32))
        return (totals, (encoded_here, grad_emb))
    start = (jnp.zeros(weight_in.shape, jnp.float32), jnp.zeros(weight_out.shape, jnp.float32))
    (grad_in, grad_out), (encoded, grad_emb) = lax.scan(per_block, start, (block_rows, segment, cot_blocks))
    grad_flat = grad_emb.reshape(TOKENS, D).astype(jnp.float32)
    table_grad = jnp.zeros((ITEMS, D), jnp.float32).at[global_row].add(jnp.where(regular[:, None], grad_flat, 0.0))
    hot_grad = jnp.zeros((HOT, D), jnp.float32).at[hot_row].add(jnp.where(regular[:, None], 0.0, grad_flat))
    return (encoded.reshape(TOKENS, D), table_grad, hot_grad, grad_in, grad_out)
```

```python
import jax
import jax.numpy as jnp
from jax import lax
from jax.experimental import pallas as pl
from jax.experimental.pallas import tpu as pltpu
from jax.sharding import PartitionSpec as P

F32 = jnp.float32
BF16 = jnp.bfloat16
I32 = jnp.int32

D = 512
HEADS = 4
HEAD_DIM = 128
LAYERS = 2
TOK = 256
N_SEQ = 16
N_COL = 8
SEQ_TOK = TOK * N_COL
CAP = 256
SLOTS = N_SEQ * CAP
ITEMS_DEV = 4096
HOT = 256
COLS = 64
CHUNK = 176
VMEM_LIMIT = 56 * 1024 * 1024

NT = (((1,), (1,)), ((), ()))
TN = (((0,), (0,)), ((), ()))


def params(**more):
    return pltpu.CompilerParams(vmem_limit_bytes=VMEM_LIMIT, **more)


def vmem(count):
    return [pl.BlockSpec(memory_space=pltpu.VMEM)] * count


SMEM = pl.BlockSpec(memory_space=pltpu.SMEM)
ANY = pl.BlockSpec(memory_space=pl.ANY)


def mm(a, b, dims=None):
    if dims is None:
        return jnp.dot(a, b, preferred_element_type=F32)
    return lax.dot_general(a, b, dims, preferred_element_type=F32)


def slot_kernel(owner_ref, item_ref, flag_ref, hot_ref, request_ref, index_ref):
    owner = owner_ref[...]
    regular = flag_ref[...] == 0
    owners = lax.broadcasted_iota(I32, (N_SEQ, SEQ_TOK), 0)
    member = jnp.where((owners == owner) & regular, 1.0, 0.0)
    member_b = member.astype(BF16)
    upper = jnp.where(
        lax.broadcasted_iota(I32, (TOK, TOK), 0) <= lax.broadcasted_iota(I32, (TOK, TOK), 1), 1.0, 0.0
    ).astype(BF16)
    carry = jnp.zeros((N_SEQ, 1), F32)
    requests = jnp.zeros((3 * N_SEQ, CAP), F32)
    item = item_ref[...]
    high = (item >> 6).astype(F32)
    low = (item & 63).astype(F32)
    for block in range(N_COL):
        span = slice(block * TOK, (block + 1) * TOK)
        here = member[:, span]
        count = mm(member_b[:, span], upper) + carry
        carry = count[:, TOK - 1 : TOK]
        slot = jnp.sum((count - 1.0) * here, axis=0, keepdims=True).astype(I32)
        place = jnp.where(
            regular[:, span], owner[:, span] * CAP + slot, SLOTS + hot_ref[:, span]
        )
        index_ref[block : block + 1, :] = place
        slots = lax.broadcasted_iota(I32, (CAP, TOK), 0)
        pick = jnp.where(slots == slot, 1.0, 0.0).astype(BF16)
        parts = jnp.concatenate([here * high[:, span], here * low[:, span], here], axis=0)
        requests += mm(parts.astype(BF16), pick, NT)
    rows = requests[:N_SEQ] * 64.0 + requests[N_SEQ : 2 * N_SEQ]
    rows = jnp.where(requests[2 * N_SEQ :] > 0.5, rows, float(ITEMS_DEV))
    request_ref[...] = rows.astype(I32)


def make_slots(owner, item, flag, hot):
    return pl.pallas_call(
        slot_kernel,
        out_shape=(
            jax.ShapeDtypeStruct((N_SEQ, CAP), I32),
            jax.ShapeDtypeStruct((N_COL, TOK), I32),
        ),
        in_specs=vmem(4),
        out_specs=tuple(vmem(2)),
        compiler_params=params(),
        name="slots",
    )(owner, item, flag, hot)


def widen(packed):
    wide = packed.astype(F32)
    return wide[:, :COLS], wide[:, COLS:]


def narrow(rows):
    return jnp.concatenate([rows[:128], rows[128:]], axis=1).astype(BF16)


def copy_rows(count, unroll, body):
    def step(i, carry):
        for u in range(unroll):
            body(i * unroll + u)
        return carry

    lax.fori_loop(0, count // unroll, step, 0)


def pick_kernel(request_ref, table_ref, out_ref, rows):
    for requester in range(N_SEQ):

        def one(slot):
            row = jnp.minimum(request_ref[requester, slot], ITEMS_DEV - 1)
            rows[pl.ds(requester * CAP + slot, 1), :] = table_ref[pl.ds(row, 1), :]

        copy_rows(CAP, 16, one)
        out_ref[requester] = narrow(rows[requester * CAP : (requester + 1) * CAP, :])


def pick_rows(requests, table):
    return pl.pallas_call(
        pick_kernel,
        out_shape=jax.ShapeDtypeStruct((N_SEQ, 128, 128), BF16),
        in_specs=[SMEM] + vmem(1),
        out_specs=vmem(1)[0],
        scratch_shapes=[pltpu.VMEM((SLOTS, COLS), F32)],
        compiler_params=params(),
        name="pick_rows",
    )(requests, table)


def place_kernel(index_ref, returned_ref, hot_ref, out_ref, source, rows):
    for owner in range(N_SEQ):
        first, second = widen(returned_ref[owner])
        source[owner * CAP : owner * CAP + 128, :] = first
        source[owner * CAP + 128 : (owner + 1) * CAP, :] = second
    source[SLOTS : SLOTS + HOT, :] = hot_ref[...].astype(F32)
    for block in range(N_COL):

        def one(token):
            rows[pl.ds(token, 1), :] = source[pl.ds(index_ref[block, token], 1), :]

        copy_rows(TOK, 16, one)
        out_ref[block] = narrow(rows[...])


def place_rows(index, returned, hot_table):
    return pl.pallas_call(
        place_kernel,
        out_shape=jax.ShapeDtypeStruct((N_COL, 128, 128), BF16),
        in_specs=[SMEM] + vmem(2),
        out_specs=vmem(1)[0],
        scratch_shapes=[pltpu.VMEM((SLOTS + HOT, COLS), F32), pltpu.VMEM((TOK, COLS), F32)],
        compiler_params=params(),
        name="place_rows",
    )(index, returned, hot_table)


def return_kernel(index_ref, grad_ref, out_ref, rows, target):
    target[...] = jnp.zeros_like(target)
    for block in range(N_COL):
        first, second = widen(grad_ref[block])
        rows[block, :128, :] = first
        rows[block, 128:, :] = second
    for block in range(N_COL):

        def one(token):
            target[pl.ds(index_ref[block, token], 1), :] = rows[block, pl.ds(token, 1), :]

        copy_rows(TOK, 16, one)
    for owner in range(N_SEQ):
        out_ref[owner] = narrow(target[owner * CAP : (owner + 1) * CAP, :])


def return_rows(index, grads):
    return pl.pallas_call(
        return_kernel,
        out_shape=jax.ShapeDtypeStruct((N_SEQ, 128, 128), BF16),
        in_specs=[SMEM] + vmem(1),
        out_specs=vmem(1)[0],
        scratch_shapes=[
            pltpu.VMEM((N_COL, TOK, COLS), F32),
            pltpu.VMEM((SLOTS + HOT, COLS), F32),
        ],
        compiler_params=params(),
        name="return_rows",
    )(index, grads)


def scatter_kernel(request_ref, incoming_ref, out_ref, rows, *totals):
    for total in totals:
        total[...] = jnp.zeros_like(total)
    for requester in range(N_SEQ):
        first, second = widen(incoming_ref[requester])
        rows[requester * CAP : requester * CAP + 128, :] = first
        rows[requester * CAP + 128 : (requester + 1) * CAP, :] = second
    part = SLOTS // len(totals)
    per = N_SEQ // len(totals)

    def step(i, carry):
        for u in range(4):
            for t, total in enumerate(totals):
                slot = i * 4 + u
                row = request_ref[t * per + slot // CAP, slot % CAP]
                total[pl.ds(row, 1), :] += rows[pl.ds(t * part + slot, 1), :]
        return carry

    lax.fori_loop(0, part // 4, step, 0)
    for block in range(ITEMS_DEV // 128):
        span = slice(block * 128, (block + 1) * 128)
        value = totals[0][span, :]
        for total in totals[1:]:
            value = value + total[span, :]
        out_ref[:, span] = value.T


def scatter_rows(requests, incoming):
    return pl.pallas_call(
        scatter_kernel,
        out_shape=jax.ShapeDtypeStruct((COLS, ITEMS_DEV), F32),
        in_specs=[SMEM] + vmem(1),
        out_specs=vmem(1)[0],
        scratch_shapes=[pltpu.VMEM((SLOTS, COLS), F32)]
        + [pltpu.VMEM((ITEMS_DEV + 8, COLS), F32)] * 4,
        compiler_params=params(),
        cost_estimate=pl.CostEstimate(flops=0, bytes_accessed=20_000_000, transcendentals=0),
        name="scatter_rows",
    )(requests, incoming).T


def norm(value):
    center = value - jnp.mean(value, axis=-1, keepdims=True)
    scale = lax.rsqrt(jnp.mean(center * center, axis=-1, keepdims=True) + 1e-05)
    return center * scale, scale


def norm_back(grad, normed, scale):
    shift = jnp.mean(grad, axis=-1, keepdims=True)
    tilt = jnp.mean(grad * normed, axis=-1, keepdims=True)
    return scale * (grad - shift - normed * tilt)


def silu_parts(value):
    gate = jax.nn.sigmoid(value)
    return value * gate, gate * (1.0 + value * (1.0 - gate))


def places():
    seq, col = lax.axis_index("seq"), lax.axis_index("col")
    y, x, core = seq & 3, col >> 1, col & 1
    return x, y, core


def stack_kernel(
    index_ref, emb_ref, win_ref, wout_ref, segment_ref, cot_ref,
    enc_ref, grad_ref, *refs
):
    outs, refs = refs[:8], refs[8:]
    stream, normed, normed_scale, proj, slope, attn, attn_slope, mixed, mixed_scale, gated, dproj, pay, sems = refs
    keep, send = outs[:4], outs[4:]
    x, y, core = places()
    col = lax.axis_index("col")

    segment = jnp.broadcast_to(segment_ref[...].astype(F32), (TOK, TOK))
    row = lax.broadcasted_iota(I32, (TOK, TOK), 0)
    column = lax.broadcasted_iota(I32, (TOK, TOK), 1)
    allowed = (segment == segment.T) & (column <= row)

    for pair in range(N_COL // 2):
        a0, a1 = widen(emb_ref[2 * pair])
        b0, b1 = widen(emb_ref[2 * pair + 1])
        lanes = slice(pair * 128, (pair + 1) * 128)
        stream[:128, lanes] = jnp.concatenate([a0, b0], axis=1)
        stream[128:, lanes] = jnp.concatenate([a1, b1], axis=1)

    def lanes_of(head):
        return slice(head * HEAD_DIM, (head + 1) * HEAD_DIM)

    scaling = HEAD_DIM ** (-0.5)
    for l in range(LAYERS):
        value, scale = norm(stream[...])
        normed[l] = value
        normed_scale[l] = scale
        rounded = value.astype(BF16)
        for part in range(4):
            pre = mm(rounded, win_ref[l, :, part * D : (part + 1) * D])
            out, tilt = silu_parts(pre)
            proj[l, part] = out.astype(BF16)
            slope[l, part] = tilt
        for head in range(HEADS):
            lanes = lanes_of(head)
            score = mm(proj[l, 2, :, lanes], proj[l, 3, :, lanes], NT) * scaling
            out, tilt = silu_parts(score)
            weight = jnp.where(allowed, out, 0.0).astype(BF16)
            attn[l, head] = weight
            attn_slope[l, head] = jnp.where(allowed, tilt * scaling, 0.0)
            mixed[l, :, lanes] = mm(weight, proj[l, 1, :, lanes])
        value, scale = norm(mixed[l])
        mixed[l] = value
        mixed_scale[l] = scale
        product = (value * proj[l, 0].astype(F32)).astype(BF16)
        gated[l] = product
        stream[...] += mm(product, wout_ref[l])
    enc_ref[...] = stream[...].astype(BF16)

    stream[...] = cot_ref[...].astype(F32)
    for l in reversed(range(LAYERS)):
        first, second = (x, y) if l == 0 else (y, x)

        def put(part, value):
            for a in range(4):
                for b in range(4):
                    chunk = 4 * a + b
                    place = 4 * ((a - first) & 3) + ((b - second) & 3)
                    pay[l, place, part * 32 : (part + 1) * 32, :] = value[chunk * 32 : (chunk + 1) * 32, :]

        grad = stream[...]
        grad_b = grad.astype(BF16)
        put(4, mm(gated[l], grad_b, TN).astype(BF16))
        dgated = mm(grad_b, wout_ref[l], NT).astype(BF16).astype(F32)
        hat = mixed[l]
        dproj[0] = ((dgated * hat).astype(BF16).astype(F32) * slope[l, 0]).astype(BF16)
        dmixed = norm_back(dgated * proj[l, 0].astype(F32), hat, mixed_scale[l]).astype(BF16)
        for head in range(HEADS):
            lanes = lanes_of(head)
            dmix = dmixed[:, lanes]
            dvalue = mm(attn[l, head], dmix, TN).astype(BF16).astype(F32)
            dproj[1, :, lanes] = (dvalue * slope[l, 1, :, lanes]).astype(BF16)
            dattn = mm(dmix, proj[l, 1, :, lanes], NT).astype(BF16).astype(F32)
            dscore = (dattn * attn_slope[l, head]).astype(BF16)
            dquery = mm(dscore, proj[l, 3, :, lanes]).astype(BF16).astype(F32)
            dproj[2, :, lanes] = (dquery * slope[l, 2, :, lanes]).astype(BF16)
            dkey = mm(dscore, proj[l, 2, :, lanes], TN).astype(BF16).astype(F32)
            dproj[3, :, lanes] = (dkey * slope[l, 3, :, lanes]).astype(BF16)
        value = normed[l]
        rounded = value.astype(BF16)
        dnormed = jnp.zeros((TOK, D), F32)
        for part in range(4):
            dpre = dproj[part]
            put(part, mm(rounded, dpre, TN).astype(BF16))
            dnormed += mm(dpre, win_ref[l, :, part * D : (part + 1) * D], NT)
        dnormed = dnormed.astype(BF16).astype(F32)
        stream[...] = grad + norm_back(dnormed, value, normed_scale[l])

    grad = stream[...]
    for pair in range(N_COL // 2):
        top = grad[:128, pair * 128 : (pair + 1) * 128]
        bottom = grad[128:, pair * 128 : (pair + 1) * 128]
        grad_ref[2 * pair] = jnp.concatenate([top[:, :COLS], bottom[:, :COLS]], axis=1).astype(BF16)
        grad_ref[2 * pair + 1] = jnp.concatenate([top[:, COLS:], bottom[:, COLS:]], axis=1).astype(BF16)
    hot_row = index_ref[pl.ds(col, 1), :] - SLOTS
    pick = jnp.where(lax.broadcasted_iota(I32, (HOT, TOK), 0) == hot_row, 1.0, 0.0).astype(BF16)
    hot_part = mm(pick, grad.astype(BF16)).astype(BF16)
    for l in range(LAYERS):
        first, second = (x, y) if l == 0 else (y, x)
        for a in range(4):
            for b in range(4):
                chunk = 4 * a + b
                place = 4 * ((a - first) & 3) + ((b - second) & 3)
                pay[l, place, 160:CHUNK, :] = hot_part[chunk * 16 : (chunk + 1) * 16, :]
    copies = []
    for a in range(4):
        for i, (outs_here, layer) in enumerate(((send, 1 - core), (keep, core))):
            copies.append(
                pltpu.make_async_copy(pay.at[layer, pl.ds(4 * a, 4)], outs_here[a], sems.at[i, a])
            )
    for copy in copies:
        copy.start()
    for copy in copies:
        copy.wait()


def run_stack(index, emb, weight_in, weight_out, segment, cotangent):
    piece = jax.ShapeDtypeStruct((4, CHUNK, D), BF16)
    return pl.pallas_call(
        stack_kernel,
        out_shape=(
            jax.ShapeDtypeStruct((TOK, D), BF16),
            jax.ShapeDtypeStruct((N_COL, 128, 128), BF16),
        )
        + (piece,) * 8,
        in_specs=vmem(6),
        out_specs=tuple(vmem(2)) + (ANY,) * 8,
        scratch_shapes=[
            pltpu.VMEM((TOK, D), F32),
            pltpu.VMEM((LAYERS, TOK, D), F32),
            pltpu.VMEM((LAYERS, TOK, 1), F32),
            pltpu.VMEM((LAYERS, 4, TOK, D), BF16),
            pltpu.VMEM((LAYERS, 4, TOK, D), F32),
            pltpu.VMEM((LAYERS, HEADS, TOK, TOK), BF16),
            pltpu.VMEM((LAYERS, HEADS, TOK, TOK), F32),
            pltpu.VMEM((LAYERS, TOK, D), F32),
            pltpu.VMEM((LAYERS, TOK, 1), F32),
            pltpu.VMEM((LAYERS, TOK, D), BF16),
            pltpu.VMEM((4, TOK, D), BF16),
            pltpu.VMEM((LAYERS, 16, CHUNK, D), BF16),
            pltpu.SemaphoreType.DMA((2, 4)),
        ],
        compiler_params=params(),
        name="layers",
    )(index, emb, weight_in, weight_out, segment, cotangent)


def device_pairs(move):
    pairs = []
    for z in range(4):
        for y in range(4):
            for x in range(4):
                for core in range(2):
                    tz, ty, tx, tcore = move(z, y, x, core)
                    pairs.append(
                        (((z * 4 + y) * 4 + x) * 2 + core, ((tz * 4 + ty) * 4 + tx) * 2 + tcore)
                    )
    return pairs


BOTH = ("seq", "col")


def to_core(value):
    return lax.ppermute(value, BOTH, device_pairs(lambda z, y, x, c: (z, y, x, 1 - c)))


def along_first(value, k):
    def move(z, y, x, c):
        return (z, y, (x + k) % 4, c) if c == 0 else (z, (y + k) % 4, x, c)

    return lax.ppermute(value, BOTH, device_pairs(move))


def along_second(value, k):
    def move(z, y, x, c):
        return (z, (y + k) % 4, x, c) if c == 0 else (z, y, (x + k) % 4, c)

    return lax.ppermute(value, BOTH, device_pairs(move))


def along_z(value, k):
    return lax.ppermute(value, BOTH, device_pairs(lambda z, y, x, c: ((z + k) % 4, y, x, c)))


def add_all(*terms):
    terms = [t.astype(F32) for t in terms]
    while len(terms) > 1:
        terms = [a + b for a, b in zip(terms[::2], terms[1::2])]
    return terms[0].astype(BF16)


def sum_everywhere(keep, send):
    order = (1, 3, 2, 0)
    got = {k: to_core(send[k]) for k in order}
    chip = {k: add_all(keep[k], got[k]) for k in order}
    came = {k: along_first(chip[k], k) for k in (1, 3, 2)}
    line = add_all(chip[0], came[2], came[1], came[3])
    came = {k: along_second(line[k], k) for k in (1, 3, 2)}
    plane = add_all(line[0], came[2], came[1], came[3])
    came = {k: along_z(plane, k) for k in (1, 3, 2)}
    total = add_all(plane, came[2], came[1], came[3])
    row = jnp.stack([total] + [along_second(total, -k) for k in (1, 2, 3)])
    mine = [row] + [along_first(row, -k) for k in (1, 2, 3)]
    other = [to_core(value) for value in mine]
    return mine, other


def finish_kernel(*refs):
    mine, other = refs[:4], refs[4:8]
    win_ref, wout_ref, hot_ref = refs[8:11]
    stage_in, stage_out, hot_rows, sems = refs[11:]
    x, y, core = places()
    col = lax.axis_index("col")
    pending = [None, None]
    step = 0
    for source, layer, own in ((mine, core, True), (other, 1 - core, False)):
        straight = layer == 0
        first = jnp.where(straight, x, y)
        second = jnp.where(straight, y, x)
        for a in range(4):
            for b in range(4):
                slot = step % 2
                if pending[slot] is not None:
                    for copy in pending[slot]:
                        copy.wait()
                chunk = 4 * ((a + first) & 3) + ((b + second) & 3)
                for part in range(4):
                    stage_in[slot, :, part * D : (part + 1) * D] = source[a][
                        b, part * 32 : (part + 1) * 32, :
                    ].astype(F32)
                stage_out[slot] = source[a][b, 128:160, :].astype(F32)
                if own:
                    hot_rows[pl.ds(pl.multiple_of(chunk * 16, 16), 16), :] = source[a][b, 160:CHUNK, :]
                rows = pl.ds(pl.multiple_of(chunk * 32, 32), 32)
                pending[slot] = [
                    pltpu.make_async_copy(stage_in.at[slot], win_ref.at[layer, rows], sems.at[slot, 0]),
                    pltpu.make_async_copy(stage_out.at[slot], wout_ref.at[layer, rows], sems.at[slot, 1]),
                ]
                for copy in pending[slot]:
                    copy.start()
                step += 1
    pick = jnp.where(
        lax.broadcasted_iota(I32, (D, COLS), 0) == lax.broadcasted_iota(I32, (D, COLS), 1) + col * COLS,
        1.0,
        0.0,
    ).astype(BF16)
    hot_ref[...] = mm(hot_rows[...], pick)
    for copies in pending:
        for copy in copies:
            copy.wait()


def finish(mine, other):
    return pl.pallas_call(
        finish_kernel,
        out_shape=(
            jax.ShapeDtypeStruct((LAYERS, D, 4 * D), F32),
            jax.ShapeDtypeStruct((LAYERS, D, D), F32),
            jax.ShapeDtypeStruct((HOT, COLS), F32),
        ),
        in_specs=vmem(8),
        out_specs=(ANY, ANY, vmem(1)[0]),
        scratch_shapes=[
            pltpu.VMEM((2, 32, 4 * D), F32),
            pltpu.VMEM((2, 32, D), F32),
            pltpu.VMEM((HOT, D), BF16),
            pltpu.SemaphoreType.DMA((2, 2)),
        ],
        compiler_params=params(),
        name="finish",
    )(*mine, *other)


def on_device(
    item_table, hot_table, weight_in, weight_out, row_owner, item_row, hot_flag, hot_row, segment, cotangent
):
    line = (1, SEQ_TOK)
    requests, index = make_slots(
        row_owner.reshape(line), item_row.reshape(line), hot_flag.reshape(line), hot_row.reshape(line)
    )
    received = lax.all_to_all(requests, "seq", split_axis=0, concat_axis=0, tiled=True)
    picked = pick_rows(received, item_table.astype(F32))
    returned = lax.all_to_all(picked, "seq", split_axis=0, concat_axis=0, tiled=True)
    placed = place_rows(index, returned, hot_table)
    emb = lax.all_to_all(placed, "col", split_axis=0, concat_axis=0, tiled=True)
    outs = run_stack(index, emb, weight_in, weight_out, segment, cotangent)
    encoded, grad_emb, keep, send = outs[0], outs[1], outs[2:6], outs[6:10]
    mine, other = sum_everywhere(keep, send)
    grad_columns = lax.all_to_all(grad_emb, "col", split_axis=0, concat_axis=0, tiled=True)
    outgoing = return_rows(index, grad_columns)
    incoming = lax.all_to_all(outgoing, "seq", split_axis=0, concat_axis=0, tiled=True)
    table_grad = scatter_rows(received, incoming)
    grad_in, grad_out, hot_grad = finish(mine, other)
    return (encoded, table_grad, hot_grad, grad_in, grad_out)


def solution(mesh):
    in_specs = (
        P("seq", "col"),
        P(None, "col"),
        P(),
        P(),
        P("seq", None),
        P("seq"),
        P("seq"),
        P("seq"),
        P(("seq", "col"), None),
        P(("seq", "col"), None),
    )
    out_specs = (P(("seq", "col"), None), P("seq", "col"), P(None, "col"), P(), P())
    return jax.shard_map(
        on_device, mesh=mesh, in_specs=in_specs, out_specs=out_specs, check_vma=False
    )
```

```python
import functools

import jax
import jax.numpy as jnp
from jax import lax
from jax.experimental import pallas as pl
from jax.experimental.pallas import tpu as pltpu
from jax.sharding import PartitionSpec as P

F32 = jnp.float32
BF16 = jnp.bfloat16
I32 = jnp.int32

D = 512
HEADS = 4
HEAD_DIM = 128
LAYERS = 2
TOK = 256
N_SEQ = 16
N_COL = 8
SEQ_TOK = TOK * N_COL
CAP = 256
SLOTS = N_SEQ * CAP
ITEMS_DEV = 4096
HOT = 256
COLS = 64
CHUNK = 176
VMEM_LIMIT = 56 * 1024 * 1024

NT = (((1,), (1,)), ((), ()))
TN = (((0,), (0,)), ((), ()))


def params(**more):
    return pltpu.CompilerParams(vmem_limit_bytes=VMEM_LIMIT, **more)


def cost(microseconds):
    return pl.CostEstimate(
        flops=int(microseconds * 1.1e9), bytes_accessed=int(microseconds * 3.6e6), transcendentals=0
    )


def vmem(count):
    return [pl.BlockSpec(memory_space=pltpu.VMEM)] * count


SMEM = pl.BlockSpec(memory_space=pltpu.SMEM)
ANY = pl.BlockSpec(memory_space=pl.ANY)


def mm(a, b, dims=None):
    if dims is None:
        return jnp.dot(a, b, preferred_element_type=F32)
    return lax.dot_general(a, b, dims, preferred_element_type=F32)


def slot_kernel(owner_ref, item_ref, flag_ref, hot_ref, request_ref, index_ref):
    owner = owner_ref[...]
    regular = flag_ref[...] == 0
    owners = lax.broadcasted_iota(I32, (N_SEQ, SEQ_TOK), 0)
    member = jnp.where((owners == owner) & regular, 1.0, 0.0)
    member_b = member.astype(BF16)
    upper = jnp.where(
        lax.broadcasted_iota(I32, (TOK, TOK), 0) <= lax.broadcasted_iota(I32, (TOK, TOK), 1), 1.0, 0.0
    ).astype(BF16)
    carry = jnp.zeros((N_SEQ, 1), F32)
    requests = jnp.zeros((3 * N_SEQ, CAP), F32)
    item = item_ref[...]
    high = (item >> 6).astype(F32)
    low = (item & 63).astype(F32)
    for block in range(N_COL):
        span = slice(block * TOK, (block + 1) * TOK)
        here = member[:, span]
        count = mm(member_b[:, span], upper) + carry
        carry = count[:, TOK - 1 : TOK]
        slot = jnp.sum((count - 1.0) * here, axis=0, keepdims=True).astype(I32)
        place = jnp.where(
            regular[:, span], owner[:, span] * CAP + slot, SLOTS + hot_ref[:, span]
        )
        index_ref[block, 0:1, :] = place[:, :128]
        index_ref[block, 1:2, :] = place[:, 128:]
        slots = lax.broadcasted_iota(I32, (CAP, TOK), 0)
        pick = jnp.where(slots == slot, 1.0, 0.0).astype(BF16)
        parts = jnp.concatenate([here * high[:, span], here * low[:, span], here], axis=0)
        requests += mm(parts.astype(BF16), pick, NT)
    rows = requests[:N_SEQ] * 64.0 + requests[N_SEQ : 2 * N_SEQ]
    rows = jnp.where(requests[2 * N_SEQ :] > 0.5, rows, float(ITEMS_DEV))
    rows = rows.astype(I32)
    request_ref[:, 0, :] = rows[:, :128]
    request_ref[:, 1, :] = rows[:, 128:]


def make_slots(owner, item, flag, hot):
    return pl.pallas_call(
        slot_kernel,
        out_shape=(
            jax.ShapeDtypeStruct((N_SEQ, 2, 128), I32),
            jax.ShapeDtypeStruct((N_COL, 2, 128), I32),
        ),
        in_specs=vmem(4),
        out_specs=tuple(vmem(2)),
        compiler_params=params(),
        cost_estimate=cost(2.5),
        name="slots",
    )(owner, item, flag, hot)


def widen(packed):
    wide = packed.astype(F32)
    return wide[:, :COLS], wide[:, COLS:]


def narrow(rows):
    return jnp.concatenate([rows[:128], rows[128:]], axis=1).astype(BF16)


def each_row(count, body, unroll=32):
    def step(i, carry):
        for u in range(unroll):
            body(i * unroll + u)
        return carry

    lax.fori_loop(0, count // unroll, step, 0)


def pick_kernel(request_ref, table_ref, out_ref, rows):
    def one(slot):
        row = jnp.minimum(request_ref[slot], ITEMS_DEV - 1)
        rows[pl.ds(slot, 1), :] = table_ref[pl.ds(row, 1), :]

    each_row(SLOTS, one)
    for requester in range(N_SEQ):
        out_ref[requester] = narrow(rows[requester * CAP : (requester + 1) * CAP, :])


def pick_rows(requests, table):
    return pl.pallas_call(
        pick_kernel,
        out_shape=jax.ShapeDtypeStruct((N_SEQ, 128, 128), BF16),
        in_specs=[SMEM] + vmem(1),
        out_specs=vmem(1)[0],
        scratch_shapes=[pltpu.VMEM((SLOTS, COLS), F32)],
        compiler_params=params(),
        cost_estimate=cost(7),
        name="pick_rows",
    )(requests.reshape(SLOTS), table)


def place_kernel(index_ref, returned_ref, hot_ref, out_ref, source, rows):
    for owner in range(N_SEQ):
        first, second = widen(returned_ref[owner])
        source[owner * CAP : owner * CAP + 128, :] = first
        source[owner * CAP + 128 : (owner + 1) * CAP, :] = second
    source[SLOTS : SLOTS + HOT, :] = hot_ref[...].astype(F32).T

    def one(token):
        rows[pl.ds(token, 1), :] = source[pl.ds(index_ref[token], 1), :]

    each_row(SEQ_TOK, one)
    for block in range(N_COL):
        out_ref[block] = narrow(rows[block * TOK : (block + 1) * TOK, :])


def place_rows(index, returned, hot_table):
    return pl.pallas_call(
        place_kernel,
        out_shape=jax.ShapeDtypeStruct((N_COL, 128, 128), BF16),
        in_specs=[SMEM] + vmem(2),
        out_specs=vmem(1)[0],
        scratch_shapes=[pltpu.VMEM((SLOTS + HOT, COLS), F32), pltpu.VMEM((SEQ_TOK, COLS), F32)],
        compiler_params=params(),
        cost_estimate=cost(4),
        name="place_rows",
    )(index.reshape(SEQ_TOK), returned, hot_table.T)


def return_kernel(index_ref, grad_ref, out_ref, rows, target):
    target[...] = jnp.zeros_like(target)
    for block in range(N_COL):
        first, second = widen(grad_ref[block])
        rows[block * TOK : block * TOK + 128, :] = first
        rows[block * TOK + 128 : (block + 1) * TOK, :] = second

    def one(token):
        target[pl.ds(index_ref[token], 1), :] = rows[pl.ds(token, 1), :]

    each_row(SEQ_TOK, one)
    for owner in range(N_SEQ):
        out_ref[owner] = narrow(target[owner * CAP : (owner + 1) * CAP, :])


def return_rows(index, grads):
    return pl.pallas_call(
        return_kernel,
        out_shape=jax.ShapeDtypeStruct((N_SEQ, 128, 128), BF16),
        in_specs=[SMEM] + vmem(1),
        out_specs=vmem(1)[0],
        scratch_shapes=[
            pltpu.VMEM((SEQ_TOK, COLS), F32),
            pltpu.VMEM((SLOTS + HOT, COLS), F32),
        ],
        compiler_params=params(),
        cost_estimate=cost(4),
        name="return_rows",
    )(index.reshape(SEQ_TOK), grads)


def scatter_kernel(request_ref, incoming_ref, out_ref, rows, *totals):
    for total in totals:
        total[...] = jnp.zeros_like(total)
    for requester in range(N_SEQ):
        first, second = widen(incoming_ref[requester])
        rows[requester * CAP : requester * CAP + 128, :] = first
        rows[requester * CAP + 128 : (requester + 1) * CAP, :] = second
    part = SLOTS // len(totals)

    def step(i, carry):
        for u in range(8):
            for t, total in enumerate(totals):
                slot = t * part + i * 8 + u
                total[pl.ds(request_ref[slot], 1), :] += rows[pl.ds(slot, 1), :]
        return carry

    lax.fori_loop(0, part // 8, step, 0)
    for block in range(ITEMS_DEV // 128):
        span = slice(block * 128, (block + 1) * 128)
        value = totals[0][span, :]
        for total in totals[1:]:
            value = value + total[span, :]
        out_ref[:, span] = value.T


def scatter_rows(requests, incoming):
    return pl.pallas_call(
        scatter_kernel,
        out_shape=jax.ShapeDtypeStruct((COLS, ITEMS_DEV), F32),
        in_specs=[SMEM] + vmem(1),
        out_specs=vmem(1)[0],
        scratch_shapes=[pltpu.VMEM((SLOTS, COLS), F32)]
        + [pltpu.VMEM((ITEMS_DEV + 8, COLS), F32)] * 4,
        compiler_params=params(),
        cost_estimate=cost(11),
        name="scatter_rows",
    )(requests.reshape(SLOTS), incoming).T


def norm(value):
    center = value - jnp.mean(value, axis=-1, keepdims=True)
    scale = lax.rsqrt(jnp.mean(center * center, axis=-1, keepdims=True) + 1e-05)
    return center * scale, scale


def norm_back(grad, normed, scale):
    shift = jnp.mean(grad, axis=-1, keepdims=True)
    tilt = jnp.mean(grad * normed, axis=-1, keepdims=True)
    return scale * (grad - shift - normed * tilt)


def silu_parts(value):
    gate = jax.nn.sigmoid(value)
    return value * gate, gate * (1.0 + value * (1.0 - gate))


def places():
    seq, col = lax.axis_index("seq"), lax.axis_index("col")
    return (col >> 1, seq & 3, seq >> 2), col & 1


def stack_kernel(
    index_ref, emb_ref, segment_ref, cot_ref, win_hbm, wout_hbm,
    enc_ref, grad_ref, *refs
):
    outs, refs = refs[:8], refs[8:]
    stream, normed, normed_scale, proj, slope, attn, attn_slope, mixed, mixed_scale, gated, dproj, pay, win_ref, wout_ref, sems, win_sems, wout_sems = refs
    keep, send = outs[:4], outs[4:]
    loads = {}
    for l in range(LAYERS):
        for part in range(4):
            span = slice(part * D, (part + 1) * D)
            loads[l, part] = pltpu.make_async_copy(
                win_hbm.at[l, :, span], win_ref.at[l, :, span], win_sems.at[l, part]
            )
        loads[l, 4] = pltpu.make_async_copy(wout_hbm.at[l], wout_ref.at[l], wout_sems.at[l])
    for l in range(LAYERS):
        for part in range(5):
            loads[l, part].start()
    (x, y, z), core = places()

    def leave(l, part, act):
        span = slice(part * 32, min(part * 32 + 32, CHUNK))

        def each(targets):
            for a in range(4):
                copy = pltpu.make_async_copy(
                    pay.at[l, 4 * a : 4 * a + 4, span], targets[a].at[:, span], sems.at[l, part, a]
                )
                getattr(copy, act)()

        pl.when(core == l)(lambda: each(keep))
        pl.when(core != l)(lambda: each(send))

    col = lax.axis_index("col")

    segment = jnp.broadcast_to(segment_ref[...].astype(F32), (TOK, TOK))
    row = lax.broadcasted_iota(I32, (TOK, TOK), 0)
    column = lax.broadcasted_iota(I32, (TOK, TOK), 1)
    allowed = (segment == segment.T) & (column <= row)

    for pair in range(N_COL // 2):
        a0, a1 = widen(emb_ref[2 * pair])
        b0, b1 = widen(emb_ref[2 * pair + 1])
        lanes = slice(pair * 128, (pair + 1) * 128)
        stream[:128, lanes] = jnp.concatenate([a0, b0], axis=1)
        stream[128:, lanes] = jnp.concatenate([a1, b1], axis=1)

    def lanes_of(head):
        return slice(head * HEAD_DIM, (head + 1) * HEAD_DIM)

    scaling = HEAD_DIM ** (-0.5)
    for l in range(LAYERS):
        value, scale = norm(stream[...])
        normed[l] = value
        normed_scale[l] = scale
        rounded = value.astype(BF16)
        for part in range(4):
            loads[l, part].wait()
            pre = mm(rounded, win_ref[l, :, part * D : (part + 1) * D])
            out, tilt = silu_parts(pre)
            proj[l, part] = out.astype(BF16)
            slope[l, part] = tilt
        for head in range(HEADS):
            lanes = lanes_of(head)
            score = mm(proj[l, 2, :, lanes], proj[l, 3, :, lanes], NT) * scaling
            out, tilt = silu_parts(score)
            weight = jnp.where(allowed, out, 0.0).astype(BF16)
            attn[l, head] = weight
            attn_slope[l, head] = jnp.where(allowed, tilt * scaling, 0.0)
            mixed[l, :, lanes] = mm(weight, proj[l, 1, :, lanes])
        value, scale = norm(mixed[l])
        mixed[l] = value
        mixed_scale[l] = scale
        product = (value * proj[l, 0].astype(F32)).astype(BF16)
        gated[l] = product
        loads[l, 4].wait()
        stream[...] += mm(product, wout_ref[l])
    enc_ref[...] = stream[...].astype(BF16)

    stream[...] = cot_ref[...].astype(F32)
    for l in reversed(range(LAYERS)):
        first, second = (x, y) if l == 0 else (y, z)

        def put(part, value):
            for a in range(4):
                for b in range(4):
                    chunk = 4 * a + b
                    place = 4 * ((a - first) & 3) + ((b - second) & 3)
                    pay[l, place, part * 32 : (part + 1) * 32, :] = value[chunk * 32 : (chunk + 1) * 32, :]
            leave(l, part, "start")

        grad = stream[...]
        grad_b = grad.astype(BF16)
        put(4, mm(gated[l], grad_b, TN).astype(BF16))
        dgated = mm(grad_b, wout_ref[l], NT).astype(BF16).astype(F32)
        hat = mixed[l]
        dproj[0] = ((dgated * hat).astype(BF16).astype(F32) * slope[l, 0]).astype(BF16)
        dmixed = norm_back(dgated * proj[l, 0].astype(F32), hat, mixed_scale[l]).astype(BF16)
        for head in range(HEADS):
            lanes = lanes_of(head)
            dmix = dmixed[:, lanes]
            dvalue = mm(attn[l, head], dmix, TN).astype(BF16).astype(F32)
            dproj[1, :, lanes] = (dvalue * slope[l, 1, :, lanes]).astype(BF16)
            dattn = mm(dmix, proj[l, 1, :, lanes], NT).astype(BF16).astype(F32)
            dscore = (dattn * attn_slope[l, head]).astype(BF16)
            dquery = mm(dscore, proj[l, 3, :, lanes]).astype(BF16).astype(F32)
            dproj[2, :, lanes] = (dquery * slope[l, 2, :, lanes]).astype(BF16)
            dkey = mm(dscore, proj[l, 2, :, lanes], TN).astype(BF16).astype(F32)
            dproj[3, :, lanes] = (dkey * slope[l, 3, :, lanes]).astype(BF16)
        value = normed[l]
        rounded = value.astype(BF16)
        dnormed = jnp.zeros((TOK, D), F32)
        for part in range(4):
            dpre = dproj[part]
            put(part, mm(rounded, dpre, TN).astype(BF16))
            dnormed += mm(dpre, win_ref[l, :, part * D : (part + 1) * D], NT)
        dnormed = dnormed.astype(BF16).astype(F32)
        stream[...] = grad + norm_back(dnormed, value, normed_scale[l])

    grad = stream[...]
    for pair in range(N_COL // 2):
        top = grad[:128, pair * 128 : (pair + 1) * 128]
        bottom = grad[128:, pair * 128 : (pair + 1) * 128]
        grad_ref[2 * pair] = jnp.concatenate([top[:, :COLS], bottom[:, :COLS]], axis=1).astype(BF16)
        grad_ref[2 * pair + 1] = jnp.concatenate([top[:, COLS:], bottom[:, COLS:]], axis=1).astype(BF16)
    hot_row = jnp.concatenate([index_ref[col, 0:1, :], index_ref[col, 1:2, :]], axis=1) - SLOTS
    pick = jnp.where(lax.broadcasted_iota(I32, (HOT, TOK), 0) == hot_row, 1.0, 0.0).astype(BF16)
    hot_part = mm(pick, grad.astype(BF16)).astype(BF16)
    for l in range(LAYERS):
        first, second = (x, y) if l == 0 else (y, z)
        for a in range(4):
            for b in range(4):
                chunk = 4 * a + b
                place = 4 * ((a - first) & 3) + ((b - second) & 3)
                pay[l, place, 160:CHUNK, :] = hot_part[chunk * 16 : (chunk + 1) * 16, :]
        leave(l, 5, "start")
    for l in range(LAYERS):
        for part in range(6):
            leave(l, part, "wait")


def run_stack(index, emb, weight_in, weight_out, segment, cotangent):
    piece = jax.ShapeDtypeStruct((4, CHUNK, D), BF16)
    return pl.pallas_call(
        stack_kernel,
        out_shape=(
            jax.ShapeDtypeStruct((TOK, D), BF16),
            jax.ShapeDtypeStruct((N_COL, 128, 128), BF16),
        )
        + (piece,) * 8,
        in_specs=vmem(4) + [ANY] * 2,
        out_specs=tuple(vmem(2)) + (ANY,) * 8,
        scratch_shapes=[
            pltpu.VMEM((TOK, D), F32),
            pltpu.VMEM((LAYERS, TOK, D), F32),
            pltpu.VMEM((LAYERS, TOK, 1), F32),
            pltpu.VMEM((LAYERS, 4, TOK, D), BF16),
            pltpu.VMEM((LAYERS, 4, TOK, D), F32),
            pltpu.VMEM((LAYERS, HEADS, TOK, TOK), BF16),
            pltpu.VMEM((LAYERS, HEADS, TOK, TOK), F32),
            pltpu.VMEM((LAYERS, TOK, D), F32),
            pltpu.VMEM((LAYERS, TOK, 1), F32),
            pltpu.VMEM((LAYERS, TOK, D), BF16),
            pltpu.VMEM((4, TOK, D), BF16),
            pltpu.VMEM((LAYERS, 16, CHUNK, D), BF16),
            pltpu.VMEM((LAYERS, D, 4 * D), BF16),
            pltpu.VMEM((LAYERS, D, D), BF16),
            pltpu.SemaphoreType.DMA((LAYERS, 6, 4)),
            pltpu.SemaphoreType.DMA((LAYERS, 4)),
            pltpu.SemaphoreType.DMA((LAYERS,)),
        ],
        compiler_params=params(),
        cost_estimate=cost(16),
        name="layers",
    )(index, emb, segment, cotangent, weight_in, weight_out)


def device_pairs(move):
    pairs = []
    for z in range(4):
        for y in range(4):
            for x in range(4):
                for core in range(2):
                    tz, ty, tx, tcore = move(z, y, x, core)
                    pairs.append(
                        (((z * 4 + y) * 4 + x) * 2 + core, ((tz * 4 + ty) * 4 + tx) * 2 + tcore)
                    )
    return pairs


BOTH = ("seq", "col")


def to_core(value):
    return lax.ppermute(value, BOTH, device_pairs(lambda z, y, x, c: (z, y, x, 1 - c)))


def along(value, stage, k):
    def move(z, y, x, c):
        place = [x, y, z]
        axis = (stage + c) % 3
        place[axis] = (place[axis] + k) % 4
        return (place[2], place[1], place[0], c)

    return lax.ppermute(value, BOTH, device_pairs(move))


def add_all(*terms):
    terms = [t.astype(F32) for t in terms]
    while len(terms) > 1:
        terms = [a + b for a, b in zip(terms[::2], terms[1::2])]
    return terms[0].astype(BF16)


def sum_everywhere(keep, send, gather_columns, send_back, exchange, scatter):
    order = (1, 3, 2, 0)
    got = {k: to_core(send[k]) for k in order}
    chip = {k: add_all(keep[k], got[k]) for k in order}
    came = {k: along(chip[k], 0, k) for k in (1, 3, 2)}
    line = add_all(chip[0], came[2], came[1], came[3])
    line, columns = lax.optimization_barrier((line, gather_columns()))
    outgoing = send_back(columns)
    came = {k: along(line[k], 1, k) for k in (1, 3, 2)}
    plane = add_all(line[0], came[2], came[1], came[3])
    came = {k: along(plane, 2, k) for k in (1, 3, 2)}
    total = add_all(plane, came[2], came[1], came[3])
    row = jnp.stack([total] + [along(total, 1, -k) for k in (1, 2, 3)])
    row, incoming = lax.optimization_barrier((row, exchange(outgoing)))
    mine = [row] + [along(row, 0, -k) for k in (1, 2, 3)]
    table_grad = scatter(incoming)
    last, table_grad = lax.optimization_barrier((mine[2], table_grad))
    other = [to_core(value) for value in (mine[0], mine[1], last, mine[3])]
    return mine, other, table_grad


def finish_kernel(own, *refs):
    sources = refs[:4]
    if own:
        win_ref, wout_ref, hot_ref, stage_in, stage_out, hot_rows, sems = refs[4:]
    else:
        win_ref, wout_ref, stage_in, stage_out, sems = refs[6:]
    (x, y, z), core = places()
    layer = core if own else 1 - core
    first = jnp.where(layer == 0, x, y)
    second = jnp.where(layer == 0, y, z)
    copies = []
    for a in range(4):
        for b in range(4):
            chunk = 4 * ((a + first) & 3) + ((b + second) & 3)
            step = 4 * a + b
            for part in range(4):
                stage_in[step, :, part * D : (part + 1) * D] = sources[a][
                    b, part * 32 : (part + 1) * 32, :
                ].astype(F32)
            stage_out[step] = sources[a][b, 128:160, :].astype(F32)
            if own:
                hot_rows[pl.ds(pl.multiple_of(chunk * 16, 16), 16), :] = sources[a][b, 160:CHUNK, :]
            rows = pl.ds(pl.multiple_of(chunk * 32, 32), 32)
            here = [
                pltpu.make_async_copy(stage_in.at[step], win_ref.at[layer, rows], sems.at[step, 0]),
                pltpu.make_async_copy(stage_out.at[step], wout_ref.at[layer, rows], sems.at[step, 1]),
            ]
            for copy in here:
                copy.start()
            copies += here
    if own:
        col = lax.axis_index("col")
        pick = jnp.where(
            lax.broadcasted_iota(I32, (COLS, D), 1) == lax.broadcasted_iota(I32, (COLS, D), 0) + col * COLS,
            1.0,
            0.0,
        ).astype(BF16)
        hot_ref[...] = mm(pick, hot_rows[...], NT)
    for copy in copies:
        copy.wait()


def finish(own, sources, *partial):
    shapes = (
        jax.ShapeDtypeStruct((LAYERS, D, 4 * D), F32),
        jax.ShapeDtypeStruct((LAYERS, D, D), F32),
    )
    scratch = [pltpu.VMEM((16, 32, 4 * D), F32), pltpu.VMEM((16, 32, D), F32)]
    if own:
        shapes += (jax.ShapeDtypeStruct((COLS, HOT), F32),)
        scratch += [pltpu.VMEM((HOT, D), BF16)]
    return pl.pallas_call(
        functools.partial(finish_kernel, own),
        out_shape=shapes,
        in_specs=vmem(4) + [ANY] * len(partial),
        out_specs=(ANY, ANY) + tuple(vmem(1) if own else ()),
        scratch_shapes=scratch + [pltpu.SemaphoreType.DMA((16, 2))],
        input_output_aliases={} if own else {4: 0, 5: 1},
        compiler_params=params(),
        cost_estimate=cost(4),
        name="finish_own" if own else "finish_other",
    )(*sources, *partial)


def on_device(
    item_table, hot_table, weight_in, weight_out, row_owner, item_row, hot_flag, hot_row, segment, cotangent
):
    line = (1, SEQ_TOK)
    requests, index = make_slots(
        row_owner.reshape(line), item_row.reshape(line), hot_flag.reshape(line), hot_row.reshape(line)
    )
    received = lax.all_to_all(requests, "seq", split_axis=0, concat_axis=0, tiled=True)
    picked = pick_rows(received, item_table.astype(F32))
    returned = lax.all_to_all(picked, "seq", split_axis=0, concat_axis=0, tiled=True)
    placed = place_rows(index, returned, hot_table)
    emb = lax.all_to_all(placed, "col", split_axis=0, concat_axis=0, tiled=True)
    outs = run_stack(index, emb, weight_in, weight_out, segment, cotangent)
    encoded, grad_emb, keep, send = outs[0], outs[1], outs[2:6], outs[6:10]

    def gather_columns():
        return lax.all_to_all(grad_emb, "col", split_axis=0, concat_axis=0, tiled=True)

    def send_back(columns):
        return return_rows(index, columns)

    def exchange(outgoing):
        return lax.all_to_all(outgoing, "seq", split_axis=0, concat_axis=0, tiled=True)

    def scatter(incoming):
        return scatter_rows(received, incoming)

    mine, other, table_grad = sum_everywhere(
        keep, send, gather_columns, send_back, exchange, scatter
    )
    grad_in, grad_out, hot_grad = finish(True, mine)
    grad_in, grad_out = finish(False, other, grad_in, grad_out)
    return (encoded, table_grad, hot_grad.T, grad_in, grad_out)


def solution(mesh):
    in_specs = (
        P("seq", "col"),
        P(None, "col"),
        P(),
        P(),
        P("seq", None),
        P("seq"),
        P("seq"),
        P("seq"),
        P(("seq", "col"), None),
        P(("seq", "col"), None),
    )
    out_specs = (P(("seq", "col"), None), P("seq", "col"), P(None, "col"), P(), P())
    return jax.shard_map(
        on_device, mesh=mesh, in_specs=in_specs, out_specs=out_specs, check_vma=False
    )
```

```python
import functools

import jax
import jax.numpy as jnp
from jax import lax
from jax.experimental import pallas as pl
from jax.experimental.pallas import tpu as pltpu
from jax.sharding import PartitionSpec as P

F32 = jnp.float32
BF16 = jnp.bfloat16
I32 = jnp.int32

D = 512
HEADS = 4
HEAD_DIM = 128
LAYERS = 2
TOK = 256
N_SEQ = 16
N_COL = 8
SEQ_TOK = TOK * N_COL
CAP = 256
SLOTS = N_SEQ * CAP
ITEMS_DEV = 4096
HOT = 256
COLS = 64
CHUNK = 176
MIB = 1024 * 1024

NT = (((1,), (1,)), ((), ()))
TN = (((0,), (0,)), ((), ()))


def params(mib):
    return pltpu.CompilerParams(vmem_limit_bytes=mib * MIB)


def cost(microseconds):
    return pl.CostEstimate(
        flops=int(microseconds * 1.1e9), bytes_accessed=int(microseconds * 3.6e6), transcendentals=0
    )


def vmem(count):
    return [pl.BlockSpec(memory_space=pltpu.VMEM)] * count


SMEM = pl.BlockSpec(memory_space=pltpu.SMEM)
ANY = pl.BlockSpec(memory_space=pl.ANY)
HBM = pl.BlockSpec(memory_space=pltpu.HBM)


def mm(a, b, dims=None):
    if dims is None:
        return jnp.dot(a, b, preferred_element_type=F32)
    return lax.dot_general(a, b, dims, preferred_element_type=F32)


def slot_kernel(owner_ref, item_ref, flag_ref, hot_ref, request_ref, index_ref):
    owner = owner_ref[...]
    regular = flag_ref[...] == 0
    owners = lax.broadcasted_iota(I32, (N_SEQ, SEQ_TOK), 0)
    member = jnp.where((owners == owner) & regular, 1.0, 0.0)
    member_b = member.astype(BF16)
    upper = jnp.where(
        lax.broadcasted_iota(I32, (TOK, TOK), 0) <= lax.broadcasted_iota(I32, (TOK, TOK), 1), 1.0, 0.0
    ).astype(BF16)
    carry = jnp.zeros((N_SEQ, 1), F32)
    requests = jnp.zeros((3 * N_SEQ, CAP), F32)
    item = item_ref[...]
    high = (item >> 6).astype(F32)
    low = (item & 63).astype(F32)
    for block in range(N_COL):
        span = slice(block * TOK, (block + 1) * TOK)
        here = member[:, span]
        count = mm(member_b[:, span], upper) + carry
        carry = count[:, TOK - 1 : TOK]
        slot = jnp.sum((count - 1.0) * here, axis=0, keepdims=True).astype(I32)
        place = jnp.where(
            regular[:, span], owner[:, span] * CAP + slot, SLOTS + hot_ref[:, span]
        )
        index_ref[block, 0:1, :] = place[:, :128]
        index_ref[block, 1:2, :] = place[:, 128:]
        slots = lax.broadcasted_iota(I32, (CAP, TOK), 0)
        pick = jnp.where(slots == slot, 1.0, 0.0).astype(BF16)
        parts = jnp.concatenate([here * high[:, span], here * low[:, span], here], axis=0)
        requests += mm(parts.astype(BF16), pick, NT)
    rows = requests[:N_SEQ] * 64.0 + requests[N_SEQ : 2 * N_SEQ]
    rows = jnp.where(requests[2 * N_SEQ :] > 0.5, rows, float(ITEMS_DEV))
    rows = rows.astype(I32)
    request_ref[:, 0, :] = rows[:, :128]
    request_ref[:, 1, :] = rows[:, 128:]


def make_slots(owner, item, flag, hot):
    return pl.pallas_call(
        slot_kernel,
        out_shape=(
            jax.ShapeDtypeStruct((N_SEQ, 2, 128), I32),
            jax.ShapeDtypeStruct((N_COL, 2, 128), I32),
        ),
        in_specs=vmem(4),
        out_specs=tuple(vmem(2)),
        compiler_params=params(60),
        cost_estimate=cost(2.5),
        name="slots",
    )(owner, item, flag, hot)


def widen(packed):
    wide = packed.astype(F32)
    return wide[:, :COLS], wide[:, COLS:]


def narrow(rows):
    return jnp.concatenate([rows[:128], rows[128:]], axis=1).astype(BF16)


def each_row(count, body, unroll=32):
    def step(i, carry):
        for u in range(unroll):
            body(i * unroll + u)
        return carry

    lax.fori_loop(0, count // unroll, step, 0)


def pick_kernel(request_ref, table_ref, out_ref, rows):
    def one(slot):
        row = jnp.minimum(request_ref[slot], ITEMS_DEV - 1)
        rows[pl.ds(slot, 1), :] = table_ref[pl.ds(row, 1), :]

    each_row(SLOTS, one)
    for requester in range(N_SEQ):
        out_ref[requester] = narrow(rows[requester * CAP : (requester + 1) * CAP, :])


def pick_rows(requests, table):
    return pl.pallas_call(
        pick_kernel,
        out_shape=jax.ShapeDtypeStruct((N_SEQ, 128, 128), BF16),
        in_specs=[SMEM] + vmem(1),
        out_specs=vmem(1)[0],
        scratch_shapes=[pltpu.VMEM((SLOTS, COLS), F32)],
        compiler_params=params(16),
        cost_estimate=cost(7),
        name="pick_rows",
    )(requests.reshape(SLOTS), table)


def place_kernel(index_ref, returned_ref, hot_ref, out_ref, source, rows):
    for owner in range(N_SEQ):
        first, second = widen(returned_ref[owner])
        source[owner * CAP : owner * CAP + 128, :] = first
        source[owner * CAP + 128 : (owner + 1) * CAP, :] = second
    source[SLOTS : SLOTS + HOT, :] = hot_ref[...].astype(F32).T

    def one(token):
        rows[pl.ds(token, 1), :] = source[pl.ds(index_ref[token], 1), :]

    each_row(SEQ_TOK, one)
    for block in range(N_COL):
        out_ref[block] = narrow(rows[block * TOK : (block + 1) * TOK, :])


def place_rows(index, returned, hot_table):
    return pl.pallas_call(
        place_kernel,
        out_shape=jax.ShapeDtypeStruct((N_COL, 128, 128), BF16),
        in_specs=[SMEM] + vmem(2),
        out_specs=vmem(1)[0],
        scratch_shapes=[pltpu.VMEM((SLOTS + HOT, COLS), F32), pltpu.VMEM((SEQ_TOK, COLS), F32)],
        compiler_params=params(16),
        cost_estimate=cost(4),
        name="place_rows",
    )(index.reshape(SEQ_TOK), returned, hot_table.T)


def return_kernel(index_ref, grad_ref, out_ref, rows, target):
    target[...] = jnp.zeros_like(target)
    for block in range(N_COL):
        first, second = widen(grad_ref[block])
        rows[block * TOK : block * TOK + 128, :] = first
        rows[block * TOK + 128 : (block + 1) * TOK, :] = second

    def one(token):
        target[pl.ds(index_ref[token], 1), :] = rows[pl.ds(token, 1), :]

    each_row(SEQ_TOK, one)
    for owner in range(N_SEQ):
        out_ref[owner] = narrow(target[owner * CAP : (owner + 1) * CAP, :])


def return_rows(index, grads):
    return pl.pallas_call(
        return_kernel,
        out_shape=jax.ShapeDtypeStruct((N_SEQ, 128, 128), BF16),
        in_specs=[SMEM] + vmem(1),
        out_specs=vmem(1)[0],
        scratch_shapes=[
            pltpu.VMEM((SEQ_TOK, COLS), F32),
            pltpu.VMEM((SLOTS + HOT, COLS), F32),
        ],
        compiler_params=params(16),
        cost_estimate=cost(4),
        name="return_rows",
    )(index.reshape(SEQ_TOK), grads)


def scatter_kernel(request_ref, incoming_ref, out_ref, rows, *totals):
    for total in totals:
        total[...] = jnp.zeros_like(total)
    for requester in range(N_SEQ):
        first, second = widen(incoming_ref[requester])
        rows[requester * CAP : requester * CAP + 128, :] = first
        rows[requester * CAP + 128 : (requester + 1) * CAP, :] = second
    part = SLOTS // len(totals)

    def step(i, carry):
        for u in range(8):
            for t, total in enumerate(totals):
                slot = t * part + i * 8 + u
                total[pl.ds(request_ref[slot], 1), :] += rows[pl.ds(slot, 1), :]
        return carry

    lax.fori_loop(0, part // 8, step, 0)
    for block in range(ITEMS_DEV // 128):
        span = slice(block * 128, (block + 1) * 128)
        value = totals[0][span, :]
        for total in totals[1:]:
            value = value + total[span, :]
        out_ref[:, span] = value.T


def scatter_rows(requests, incoming):
    return pl.pallas_call(
        scatter_kernel,
        out_shape=jax.ShapeDtypeStruct((COLS, ITEMS_DEV), F32),
        in_specs=[SMEM] + vmem(1),
        out_specs=vmem(1)[0],
        scratch_shapes=[pltpu.VMEM((SLOTS, COLS), F32)]
        + [pltpu.VMEM((ITEMS_DEV + 8, COLS), F32)] * 4,
        compiler_params=params(24),
        cost_estimate=cost(11),
        name="scatter_rows",
    )(requests.reshape(SLOTS), incoming).T


def norm(value):
    center = value - jnp.mean(value, axis=-1, keepdims=True)
    scale = lax.rsqrt(jnp.mean(center * center, axis=-1, keepdims=True) + 1e-05)
    return center * scale, scale


def norm_back(grad, normed, scale):
    shift = jnp.mean(grad, axis=-1, keepdims=True)
    tilt = jnp.mean(grad * normed, axis=-1, keepdims=True)
    return scale * (grad - shift - normed * tilt)


def silu_parts(value):
    gate = jax.nn.sigmoid(value)
    return value * gate, gate * (1.0 + value * (1.0 - gate))


def places():
    seq, col = lax.axis_index("seq"), lax.axis_index("col")
    return (col >> 1, seq & 3, seq >> 2), col & 1


def stack_kernel(
    index_ref, emb_ref, segment_ref, cot_ref, win_ref, wout_ref,
    enc_ref, grad_ref, *refs
):
    outs, refs = refs[:8], refs[8:]
    stream, normed, normed_scale, proj, slope, attn, attn_slope, mixed, mixed_scale, gated, dproj, pay, sems = refs
    keep, send = outs[:4], outs[4:]
    (x, y, z), core = places()

    def leave(l, span, sem, act):
        def each(targets):
            for a in range(4):
                copy = pltpu.make_async_copy(
                    pay.at[l, 4 * a : 4 * a + 4, span], targets[a].at[:, span], sems.at[sem, a]
                )
                getattr(copy, act)()

        pl.when(core == l)(lambda: each(keep))
        pl.when(core != l)(lambda: each(send))

    moves = ((1, slice(0, 160), 0), (1, slice(160, CHUNK), 1), (0, slice(0, CHUNK), 2))
    col = lax.axis_index("col")

    segment = jnp.broadcast_to(segment_ref[...].astype(F32), (TOK, TOK))
    row = lax.broadcasted_iota(I32, (TOK, TOK), 0)
    column = lax.broadcasted_iota(I32, (TOK, TOK), 1)
    allowed = (segment == segment.T) & (column <= row)

    for pair in range(N_COL // 2):
        a0, a1 = widen(emb_ref[2 * pair])
        b0, b1 = widen(emb_ref[2 * pair + 1])
        lanes = slice(pair * 128, (pair + 1) * 128)
        stream[:128, lanes] = jnp.concatenate([a0, b0], axis=1)
        stream[128:, lanes] = jnp.concatenate([a1, b1], axis=1)

    def lanes_of(head):
        return slice(head * HEAD_DIM, (head + 1) * HEAD_DIM)

    scaling = HEAD_DIM ** (-0.5)
    for l in range(LAYERS):
        value, scale = norm(stream[...])
        normed[l] = value
        normed_scale[l] = scale
        rounded = value.astype(BF16)
        for part in range(4):
            pre = mm(rounded, win_ref[l, :, part * D : (part + 1) * D])
            out, tilt = silu_parts(pre)
            proj[l, part] = out.astype(BF16)
            slope[l, part] = tilt
        for head in range(HEADS):
            lanes = lanes_of(head)
            score = mm(proj[l, 2, :, lanes], proj[l, 3, :, lanes], NT) * scaling
            out, tilt = silu_parts(score)
            weight = jnp.where(allowed, out, 0.0).astype(BF16)
            attn[l, head] = weight
            attn_slope[l, head] = jnp.where(allowed, tilt * scaling, 0.0)
            mixed[l, :, lanes] = mm(weight, proj[l, 1, :, lanes])
        value, scale = norm(mixed[l])
        mixed[l] = value
        mixed_scale[l] = scale
        product = (value * proj[l, 0].astype(F32)).astype(BF16)
        gated[l] = product
        stream[...] += mm(product, wout_ref[l])
    enc_ref[...] = stream[...].astype(BF16)

    stream[...] = cot_ref[...].astype(F32)
    for l in reversed(range(LAYERS)):
        first, second = (x, y) if l == 0 else (y, z)

        def put(part, value):
            for a in range(4):
                for b in range(4):
                    chunk = 4 * a + b
                    place = 4 * ((a - first) & 3) + ((b - second) & 3)
                    pay[l, place, part * 32 : (part + 1) * 32, :] = value[chunk * 32 : (chunk + 1) * 32, :]

        grad = stream[...]
        grad_b = grad.astype(BF16)
        put(4, mm(gated[l], grad_b, TN).astype(BF16))
        dgated = mm(grad_b, wout_ref[l], NT).astype(BF16).astype(F32)
        hat = mixed[l]
        dproj[0] = ((dgated * hat).astype(BF16).astype(F32) * slope[l, 0]).astype(BF16)
        dmixed = norm_back(dgated * proj[l, 0].astype(F32), hat, mixed_scale[l]).astype(BF16)
        for head in range(HEADS):
            lanes = lanes_of(head)
            dmix = dmixed[:, lanes]
            dvalue = mm(attn[l, head], dmix, TN).astype(BF16).astype(F32)
            dproj[1, :, lanes] = (dvalue * slope[l, 1, :, lanes]).astype(BF16)
            dattn = mm(dmix, proj[l, 1, :, lanes], NT).astype(BF16).astype(F32)
            dscore = (dattn * attn_slope[l, head]).astype(BF16)
            dquery = mm(dscore, proj[l, 3, :, lanes]).astype(BF16).astype(F32)
            dproj[2, :, lanes] = (dquery * slope[l, 2, :, lanes]).astype(BF16)
            dkey = mm(dscore, proj[l, 2, :, lanes], TN).astype(BF16).astype(F32)
            dproj[3, :, lanes] = (dkey * slope[l, 3, :, lanes]).astype(BF16)
        value = normed[l]
        rounded = value.astype(BF16)
        dnormed = jnp.zeros((TOK, D), F32)
        for part in range(4):
            dpre = dproj[part]
            put(part, mm(rounded, dpre, TN).astype(BF16))
            dnormed += mm(dpre, win_ref[l, :, part * D : (part + 1) * D], NT)
        dnormed = dnormed.astype(BF16).astype(F32)
        stream[...] = grad + norm_back(dnormed, value, normed_scale[l])
        if l == 1:
            leave(*moves[0], "start")

    grad = stream[...]
    for pair in range(N_COL // 2):
        top = grad[:128, pair * 128 : (pair + 1) * 128]
        bottom = grad[128:, pair * 128 : (pair + 1) * 128]
        grad_ref[2 * pair] = jnp.concatenate([top[:, :COLS], bottom[:, :COLS]], axis=1).astype(BF16)
        grad_ref[2 * pair + 1] = jnp.concatenate([top[:, COLS:], bottom[:, COLS:]], axis=1).astype(BF16)
    hot_row = jnp.concatenate([index_ref[col, 0:1, :], index_ref[col, 1:2, :]], axis=1) - SLOTS
    pick = jnp.where(lax.broadcasted_iota(I32, (HOT, TOK), 0) == hot_row, 1.0, 0.0).astype(BF16)
    hot_part = mm(pick, grad.astype(BF16)).astype(BF16)
    for l in range(LAYERS):
        first, second = (x, y) if l == 0 else (y, z)
        for a in range(4):
            for b in range(4):
                chunk = 4 * a + b
                place = 4 * ((a - first) & 3) + ((b - second) & 3)
                pay[l, place, 160:CHUNK, :] = hot_part[chunk * 16 : (chunk + 1) * 16, :]
    for move in moves[1:]:
        leave(*move, "start")
    for move in moves:
        leave(*move, "wait")


def run_stack(index, emb, weight_in, weight_out, segment, cotangent):
    piece = jax.ShapeDtypeStruct((4, CHUNK, D), BF16)
    return pl.pallas_call(
        stack_kernel,
        out_shape=(
            jax.ShapeDtypeStruct((TOK, D), BF16),
            jax.ShapeDtypeStruct((N_COL, 128, 128), BF16),
        )
        + (piece,) * 8,
        in_specs=vmem(6),
        out_specs=tuple(vmem(2)) + (HBM,) * 8,
        scratch_shapes=[
            pltpu.VMEM((TOK, D), F32),
            pltpu.VMEM((LAYERS, TOK, D), F32),
            pltpu.VMEM((LAYERS, TOK, 1), F32),
            pltpu.VMEM((LAYERS, 4, TOK, D), BF16),
            pltpu.VMEM((LAYERS, 4, TOK, D), F32),
            pltpu.VMEM((LAYERS, HEADS, TOK, TOK), BF16),
            pltpu.VMEM((LAYERS, HEADS, TOK, TOK), F32),
            pltpu.VMEM((LAYERS, TOK, D), F32),
            pltpu.VMEM((LAYERS, TOK, 1), F32),
            pltpu.VMEM((LAYERS, TOK, D), BF16),
            pltpu.VMEM((4, TOK, D), BF16),
            pltpu.VMEM((LAYERS, 16, CHUNK, D), BF16),
            pltpu.SemaphoreType.DMA((3, 4)),
        ],
        compiler_params=params(36),
        cost_estimate=cost(16),
        name="layers",
    )(index, emb, segment, cotangent, weight_in, weight_out)


def device_pairs(move):
    pairs = []
    for z in range(4):
        for y in range(4):
            for x in range(4):
                for core in range(2):
                    tz, ty, tx, tcore = move(z, y, x, core)
                    pairs.append(
                        (((z * 4 + y) * 4 + x) * 2 + core, ((tz * 4 + ty) * 4 + tx) * 2 + tcore)
                    )
    return pairs


BOTH = ("seq", "col")


def to_core(value):
    return lax.ppermute(value, BOTH, device_pairs(lambda z, y, x, c: (z, y, x, 1 - c)))


def along(value, stage, k):
    def move(z, y, x, c):
        place = [x, y, z]
        axis = (stage + c) % 3
        place[axis] = (place[axis] + k) % 4
        return (place[2], place[1], place[0], c)

    return lax.ppermute(value, BOTH, device_pairs(move))


def add_all(*terms):
    terms = [t.astype(F32) for t in terms]
    while len(terms) > 1:
        terms = [a + b for a, b in zip(terms[::2], terms[1::2])]
    return terms[0].astype(BF16)


def sum_everywhere(keep, send, grad_emb, gather_columns, send_back, exchange, scatter):
    order = (2, 1, 3, 0)
    got = {k: to_core(send[k]) for k in order}
    chip = {k: add_all(keep[k], got[k]) for k in order}
    came = {k: along(chip[k], 0, k) for k in (2, 1, 3)}
    line = add_all(chip[0], came[2], came[1], came[3])
    line, grad_emb = lax.optimization_barrier((line, grad_emb))
    came = {k: along(line[k], 1, k) for k in (2, 1, 3)}
    plane = add_all(line[0], came[2], came[1], came[3])
    outgoing = send_back(gather_columns(grad_emb))
    came = {k: along(plane, 2, k) for k in (2, 1, 3)}
    total = add_all(plane, came[2], came[1], came[3])
    row = jnp.stack([total] + [along(total, 1, -k) for k in (1, 2, 3)])
    incoming = exchange(outgoing)
    mine = {k: along(row, 0, -k) for k in (2, 1, 3)}
    mine[0] = row
    other = {0: to_core(row)}
    table_grad = scatter(incoming)
    grads = finish([row, other[0]], [(0, True), (0, False)])
    pieces = lax.optimization_barrier((mine[1], mine[2], mine[3], table_grad, grads))
    mine[1], mine[2], mine[3], table_grad, grads = pieces
    other.update({k: to_core(mine[k]) for k in (1, 2, 3)})
    grads = finish([mine[k] for k in (1, 2, 3)], [(k, True) for k in (1, 2, 3)], grads)
    hot_grad = hot_sums([mine[k] for k in range(4)])
    grads = finish([other[k] for k in (1, 2, 3)], [(k, False) for k in (1, 2, 3)], grads)
    return grads[0], grads[1], hot_grad, table_grad


def finish_kernel(pieces, start, *refs):
    sources, refs = refs[: len(pieces)], refs[len(pieces) :]
    win_ref, wout_ref, stage_in, stage_out, sems = refs if start else refs[2:]
    (x, y, z), core = places()
    copies = []
    for i, (a, own) in enumerate(pieces):
        layer = core if own else 1 - core
        first = jnp.where(layer == 0, x, y)
        second = jnp.where(layer == 0, y, z)
        for b in range(4):
            chunk = 4 * ((a + first) & 3) + ((b + second) & 3)
            step = 4 * i + b
            for part in range(4):
                stage_in[step, :, part * D : (part + 1) * D] = sources[i][
                    b, part * 32 : (part + 1) * 32, :
                ].astype(F32)
            stage_out[step] = sources[i][b, 128:160, :].astype(F32)
            rows = pl.ds(pl.multiple_of(chunk * 32, 32), 32)
            here = [
                pltpu.make_async_copy(stage_in.at[step], win_ref.at[layer, rows], sems.at[step, 0]),
                pltpu.make_async_copy(stage_out.at[step], wout_ref.at[layer, rows], sems.at[step, 1]),
            ]
            for copy in here:
                copy.start()
            copies += here
    for copy in copies:
        copy.wait()


def finish(sources, pieces, partial=()):
    steps = 4 * len(pieces)
    return pl.pallas_call(
        functools.partial(finish_kernel, pieces, not partial),
        out_shape=(
            jax.ShapeDtypeStruct((LAYERS, D, 4 * D), F32),
            jax.ShapeDtypeStruct((LAYERS, D, D), F32),
        ),
        in_specs=vmem(len(pieces)) + [ANY] * len(partial),
        out_specs=(ANY, ANY),
        scratch_shapes=[
            pltpu.VMEM((steps, 32, 4 * D), F32),
            pltpu.VMEM((steps, 32, D), F32),
            pltpu.SemaphoreType.DMA((steps, 2)),
        ],
        input_output_aliases={len(pieces): 0, len(pieces) + 1: 1} if partial else {},
        compiler_params=params(6 + 3 * len(pieces)),
        cost_estimate=cost(0.5 + 0.6 * len(pieces)),
        name="widen_sums",
    )(*sources, *partial)


def hot_kernel(*refs):
    sources, hot_ref, rows = refs[:4], refs[4], refs[5]
    (x, y, z), core = places()
    col = lax.axis_index("col")
    first = jnp.where(core == 0, x, y)
    second = jnp.where(core == 0, y, z)
    for a in range(4):
        for b in range(4):
            chunk = 4 * ((a + first) & 3) + ((b + second) & 3)
            rows[pl.ds(pl.multiple_of(chunk * 16, 16), 16), :] = sources[a][b]
    pick = jnp.where(
        lax.broadcasted_iota(I32, (COLS, D), 1) == lax.broadcasted_iota(I32, (COLS, D), 0) + col * COLS,
        1.0,
        0.0,
    ).astype(BF16)
    hot_ref[...] = mm(pick, rows[...], NT)


def hot_sums(mine):
    return pl.pallas_call(
        hot_kernel,
        out_shape=jax.ShapeDtypeStruct((COLS, HOT), F32),
        in_specs=vmem(4),
        out_specs=vmem(1)[0],
        scratch_shapes=[pltpu.VMEM((HOT, D), BF16)],
        compiler_params=params(8),
        cost_estimate=cost(1),
        name="hot_sums",
    )(*[value[:, 160:CHUNK] for value in mine]).T


def on_device(
    item_table, hot_table, weight_in, weight_out, row_owner, item_row, hot_flag, hot_row, segment, cotangent
):
    line = (1, SEQ_TOK)
    requests, index = make_slots(
        row_owner.reshape(line), item_row.reshape(line), hot_flag.reshape(line), hot_row.reshape(line)
    )
    received = lax.all_to_all(requests, "seq", split_axis=0, concat_axis=0, tiled=True)
    picked = pick_rows(received, item_table.astype(F32))
    returned = lax.all_to_all(picked, "seq", split_axis=0, concat_axis=0, tiled=True)
    placed = place_rows(index, returned, hot_table)
    emb = lax.all_to_all(placed, "col", split_axis=0, concat_axis=0, tiled=True)
    outs = run_stack(index, emb, weight_in, weight_out, segment, cotangent)
    encoded, grad_emb, keep, send = outs[0], outs[1], outs[2:6], outs[6:10]

    def gather_columns(grad_emb):
        return lax.all_to_all(grad_emb, "col", split_axis=0, concat_axis=0, tiled=True)

    def send_back(columns):
        return return_rows(index, columns)

    def exchange(outgoing):
        return lax.all_to_all(outgoing, "seq", split_axis=0, concat_axis=0, tiled=True)

    def scatter(incoming):
        return scatter_rows(received, incoming)

    grad_in, grad_out, hot_grad, table_grad = sum_everywhere(
        keep, send, grad_emb, gather_columns, send_back, exchange, scatter
    )
    return (encoded, table_grad, hot_grad, grad_in, grad_out)


def solution(mesh):
    in_specs = (
        P("seq", "col"),
        P(None, "col"),
        P(),
        P(),
        P("seq", None),
        P("seq"),
        P("seq"),
        P("seq"),
        P(("seq", "col"), None),
        P(("seq", "col"), None),
    )
    out_specs = (P(("seq", "col"), None), P("seq", "col"), P(None, "col"), P(), P())
    return jax.shard_map(
        on_device, mesh=mesh, in_specs=in_specs, out_specs=out_specs, check_vma=False
    )
```

```python
import functools

import jax
import jax.numpy as jnp
from jax import lax
from jax.experimental import pallas as pl
from jax.experimental.pallas import tpu as pltpu
from jax.sharding import PartitionSpec as P

F32 = jnp.float32
BF16 = jnp.bfloat16
I32 = jnp.int32

D = 512
HEADS = 4
HEAD_DIM = 128
LAYERS = 2
TOK = 256
N_SEQ = 16
N_COL = 8
SEQ_TOK = TOK * N_COL
CAP = 256
SLOTS = N_SEQ * CAP
ITEMS_DEV = 4096
HOT = 256
COLS = 64
CHUNK = 176
MIB = 1024 * 1024

NT = (((1,), (1,)), ((), ()))
TN = (((0,), (0,)), ((), ()))


def params(mib):
    return pltpu.CompilerParams(vmem_limit_bytes=mib * MIB)


def cost(microseconds):
    return pl.CostEstimate(
        flops=int(microseconds * 1.1e9), bytes_accessed=int(microseconds * 3.6e6), transcendentals=0
    )


def vmem(count):
    return [pl.BlockSpec(memory_space=pltpu.VMEM)] * count


SMEM = pl.BlockSpec(memory_space=pltpu.SMEM)
ANY = pl.BlockSpec(memory_space=pl.ANY)
HBM = pl.BlockSpec(memory_space=pltpu.HBM)


def mm(a, b, dims=None):
    if dims is None:
        return jnp.dot(a, b, preferred_element_type=F32)
    return lax.dot_general(a, b, dims, preferred_element_type=F32)


def slot_kernel(owner_ref, item_ref, flag_ref, hot_ref, request_ref, index_ref):
    owner = owner_ref[...]
    regular = flag_ref[...] == 0
    owners = lax.broadcasted_iota(I32, (N_SEQ, SEQ_TOK), 0)
    member = jnp.where((owners == owner) & regular, 1.0, 0.0)
    member_b = member.astype(BF16)
    upper = jnp.where(
        lax.broadcasted_iota(I32, (TOK, TOK), 0) <= lax.broadcasted_iota(I32, (TOK, TOK), 1), 1.0, 0.0
    ).astype(BF16)
    carry = jnp.zeros((N_SEQ, 1), F32)
    requests = jnp.zeros((3 * N_SEQ, CAP), F32)
    item = item_ref[...]
    high = (item >> 6).astype(F32)
    low = (item & 63).astype(F32)
    for block in range(N_COL):
        span = slice(block * TOK, (block + 1) * TOK)
        here = member[:, span]
        count = mm(member_b[:, span], upper) + carry
        carry = count[:, TOK - 1 : TOK]
        slot = jnp.sum((count - 1.0) * here, axis=0, keepdims=True).astype(I32)
        place = jnp.where(
            regular[:, span], owner[:, span] * CAP + slot, SLOTS + hot_ref[:, span]
        )
        index_ref[block, 0:1, :] = place[:, :128]
        index_ref[block, 1:2, :] = place[:, 128:]
        slots = lax.broadcasted_iota(I32, (CAP, TOK), 0)
        pick = jnp.where(slots == slot, 1.0, 0.0).astype(BF16)
        parts = jnp.concatenate([here * high[:, span], here * low[:, span], here], axis=0)
        requests += mm(parts.astype(BF16), pick, NT)
    rows = requests[:N_SEQ] * 64.0 + requests[N_SEQ : 2 * N_SEQ]
    rows = jnp.where(requests[2 * N_SEQ :] > 0.5, rows, float(ITEMS_DEV))
    rows = rows.astype(I32)
    request_ref[:, 0, :] = rows[:, :128]
    request_ref[:, 1, :] = rows[:, 128:]


def make_slots(owner, item, flag, hot):
    return pl.pallas_call(
        slot_kernel,
        out_shape=(
            jax.ShapeDtypeStruct((N_SEQ, 2, 128), I32),
            jax.ShapeDtypeStruct((N_COL, 2, 128), I32),
        ),
        in_specs=vmem(4),
        out_specs=tuple(vmem(2)),
        compiler_params=params(60),
        cost_estimate=cost(2.5),
        name="slots",
    )(owner, item, flag, hot)


def widen(packed):
    wide = packed.astype(F32)
    return wide[:, :COLS], wide[:, COLS:]


def narrow(rows):
    return jnp.concatenate([rows[:128], rows[128:]], axis=1).astype(BF16)


def each_row(count, body, unroll=32):
    def step(i, carry):
        for u in range(unroll):
            body(i * unroll + u)
        return carry

    lax.fori_loop(0, count // unroll, step, 0)


GROUP = 32


def pick_kernel(request_ref, table_ref, out_ref, rows):
    def group(i, carry):
        start = i * GROUP

        @pl.when(request_ref[start] < ITEMS_DEV)
        def asked():
            for u in range(GROUP):
                rows[pl.ds(start + u, 1), :] = table_ref[pl.ds(request_ref[start + u], 1), :]

        return carry

    lax.fori_loop(0, SLOTS // GROUP, group, 0)
    for requester in range(N_SEQ):
        out_ref[requester] = narrow(rows[requester * CAP : (requester + 1) * CAP, :])


def pick_rows(requests, table):
    return pl.pallas_call(
        pick_kernel,
        out_shape=jax.ShapeDtypeStruct((N_SEQ, 128, 128), BF16),
        in_specs=[SMEM] + vmem(1),
        out_specs=vmem(1)[0],
        scratch_shapes=[pltpu.VMEM((SLOTS, COLS), F32)],
        compiler_params=params(16),
        cost_estimate=cost(7),
        name="pick_rows",
    )(requests.reshape(SLOTS), table)


def place_kernel(index_ref, returned_ref, hot_ref, out_ref, source, rows):
    for owner in range(N_SEQ):
        first, second = widen(returned_ref[owner])
        source[owner * CAP : owner * CAP + 128, :] = first
        source[owner * CAP + 128 : (owner + 1) * CAP, :] = second
    source[SLOTS : SLOTS + HOT, :] = hot_ref[...].astype(F32).T

    def one(token):
        rows[pl.ds(token, 1), :] = source[pl.ds(index_ref[token], 1), :]

    each_row(SEQ_TOK, one)
    for block in range(N_COL):
        out_ref[block] = narrow(rows[block * TOK : (block + 1) * TOK, :])


def place_rows(index, returned, hot_table):
    return pl.pallas_call(
        place_kernel,
        out_shape=jax.ShapeDtypeStruct((N_COL, 128, 128), BF16),
        in_specs=[SMEM] + vmem(2),
        out_specs=vmem(1)[0],
        scratch_shapes=[pltpu.VMEM((SLOTS + HOT, COLS), F32), pltpu.VMEM((SEQ_TOK, COLS), F32)],
        compiler_params=params(16),
        cost_estimate=cost(4),
        name="place_rows",
    )(index.reshape(SEQ_TOK), returned, hot_table.T)


def return_kernel(index_ref, grad_ref, out_ref, rows, target):
    target[...] = jnp.zeros_like(target)
    for block in range(N_COL):
        first, second = widen(grad_ref[block])
        rows[block * TOK : block * TOK + 128, :] = first
        rows[block * TOK + 128 : (block + 1) * TOK, :] = second

    def one(token):
        target[pl.ds(index_ref[token], 1), :] = rows[pl.ds(token, 1), :]

    each_row(SEQ_TOK, one)
    for owner in range(N_SEQ):
        out_ref[owner] = narrow(target[owner * CAP : (owner + 1) * CAP, :])


def return_rows(index, grads):
    return pl.pallas_call(
        return_kernel,
        out_shape=jax.ShapeDtypeStruct((N_SEQ, 128, 128), BF16),
        in_specs=[SMEM] + vmem(1),
        out_specs=vmem(1)[0],
        scratch_shapes=[
            pltpu.VMEM((SEQ_TOK, COLS), F32),
            pltpu.VMEM((SLOTS + HOT, COLS), F32),
        ],
        compiler_params=params(16),
        cost_estimate=cost(4),
        name="return_rows",
    )(index.reshape(SEQ_TOK), grads)


def scatter_kernel(request_ref, incoming_ref, out_ref, rows, *totals):
    for total in totals:
        total[...] = jnp.zeros_like(total)
    for requester in range(N_SEQ):
        first, second = widen(incoming_ref[requester])
        rows[requester * CAP : requester * CAP + 128, :] = first
        rows[requester * CAP + 128 : (requester + 1) * CAP, :] = second
    part = SLOTS // len(totals)

    def group(i, carry):
        starts = [t * part + i * 8 for t in range(len(totals))]
        held = [request_ref[start] < ITEMS_DEV for start in starts]

        @pl.when(functools.reduce(jnp.logical_or, held))
        def some():
            for u in range(8):
                for start, total in zip(starts, totals):
                    slot = start + u
                    total[pl.ds(request_ref[slot], 1), :] += rows[pl.ds(slot, 1), :]

        return carry

    lax.fori_loop(0, part // 8, group, 0)
    for block in range(ITEMS_DEV // 128):
        span = slice(block * 128, (block + 1) * 128)
        value = totals[0][span, :]
        for total in totals[1:]:
            value = value + total[span, :]
        out_ref[:, span] = value.T


def scatter_rows(requests, incoming):
    return pl.pallas_call(
        scatter_kernel,
        out_shape=jax.ShapeDtypeStruct((COLS, ITEMS_DEV), F32),
        in_specs=[SMEM] + vmem(1),
        out_specs=vmem(1)[0],
        scratch_shapes=[pltpu.VMEM((SLOTS, COLS), F32)]
        + [pltpu.VMEM((ITEMS_DEV + 8, COLS), F32)] * 4,
        compiler_params=params(24),
        cost_estimate=cost(11),
        name="scatter_rows",
    )(requests.reshape(SLOTS), incoming).T


def norm(value):
    center = value - jnp.mean(value, axis=-1, keepdims=True)
    scale = lax.rsqrt(jnp.mean(center * center, axis=-1, keepdims=True) + 1e-05)
    return center * scale, scale


def norm_back(grad, normed, scale):
    shift = jnp.mean(grad, axis=-1, keepdims=True)
    tilt = jnp.mean(grad * normed, axis=-1, keepdims=True)
    return scale * (grad - shift - normed * tilt)


def silu_parts(value):
    gate = jax.nn.sigmoid(value)
    return value * gate, gate * (1.0 + value * (1.0 - gate))


def places():
    seq, col = lax.axis_index("seq"), lax.axis_index("col")
    return (col >> 1, seq & 3, seq >> 2), col & 1


def stack_kernel(
    index_ref, emb_ref, segment_ref, cot_ref, win_ref, wout_ref,
    enc_ref, grad_ref, *refs
):
    outs, refs = refs[:8], refs[8:]
    stream, normed, normed_scale, proj, slope, attn, attn_slope, mixed, mixed_scale, gated, dproj, pay, sems = refs
    keep, send = outs[:4], outs[4:]
    (x, y, z), core = places()

    def leave(l, span, sem, act):
        def each(targets):
            for a in range(4):
                copy = pltpu.make_async_copy(
                    pay.at[l, 4 * a : 4 * a + 4, span], targets[a].at[:, span], sems.at[sem, a]
                )
                getattr(copy, act)()

        pl.when(core == l)(lambda: each(keep))
        pl.when(core != l)(lambda: each(send))

    moves = tuple((l, span, i) for i, (l, span) in enumerate(
        ((1, slice(0, 160)), (0, slice(0, 160)), (1, slice(160, CHUNK)), (0, slice(160, CHUNK)))
    ))
    col = lax.axis_index("col")

    segment = jnp.broadcast_to(segment_ref[...].astype(F32), (TOK, TOK))
    row = lax.broadcasted_iota(I32, (TOK, TOK), 0)
    column = lax.broadcasted_iota(I32, (TOK, TOK), 1)
    allowed = (segment == segment.T) & (column <= row)

    for pair in range(N_COL // 2):
        a0, a1 = widen(emb_ref[2 * pair])
        b0, b1 = widen(emb_ref[2 * pair + 1])
        lanes = slice(pair * 128, (pair + 1) * 128)
        stream[:128, lanes] = jnp.concatenate([a0, b0], axis=1)
        stream[128:, lanes] = jnp.concatenate([a1, b1], axis=1)

    def lanes_of(head):
        return slice(head * HEAD_DIM, (head + 1) * HEAD_DIM)

    scaling = HEAD_DIM ** (-0.5)
    for l in range(LAYERS):
        value, scale = norm(stream[...])
        normed[l] = value
        normed_scale[l] = scale
        rounded = value.astype(BF16)
        for part in (2, 3, 1, 0):
            pre = mm(rounded, win_ref[l, :, part * D : (part + 1) * D])
            out, tilt = silu_parts(pre)
            proj[l, part] = out.astype(BF16)
            slope[l, part] = tilt
        scores = [mm(proj[l, 2, :, lanes_of(h)], proj[l, 3, :, lanes_of(h)], NT) for h in range(HEADS)]
        for head in range(HEADS):
            lanes = lanes_of(head)
            out, tilt = silu_parts(scores[head] * scaling)
            weight = jnp.where(allowed, out, 0.0).astype(BF16)
            attn[l, head] = weight
            attn_slope[l, head] = jnp.where(allowed, tilt * scaling, 0.0)
            mixed[l, :, lanes] = mm(weight, proj[l, 1, :, lanes])
        value, scale = norm(mixed[l])
        mixed[l] = value
        mixed_scale[l] = scale
        product = (value * proj[l, 0].astype(F32)).astype(BF16)
        gated[l] = product
        stream[...] += mm(product, wout_ref[l])
    enc_ref[...] = stream[...].astype(BF16)

    stream[...] = cot_ref[...].astype(F32)
    for l in reversed(range(LAYERS)):
        first, second = (x, y) if l == 0 else (y, z)

        def put(part, value):
            for a in range(4):
                for b in range(4):
                    chunk = 4 * a + b
                    place = 4 * ((a - first) & 3) + ((b - second) & 3)
                    pay[l, place, part * 32 : (part + 1) * 32, :] = value[chunk * 32 : (chunk + 1) * 32, :]

        grad = stream[...]
        grad_b = grad.astype(BF16)
        put(4, mm(gated[l], grad_b, TN).astype(BF16))
        dgated = mm(grad_b, wout_ref[l], NT).astype(BF16).astype(F32)
        hat = mixed[l]
        dproj[0] = ((dgated * hat).astype(BF16).astype(F32) * slope[l, 0]).astype(BF16)
        dmixed = norm_back(dgated * proj[l, 0].astype(F32), hat, mixed_scale[l]).astype(BF16)
        heads = [lanes_of(h) for h in range(HEADS)]
        dmixes = [dmixed[:, lanes] for lanes in heads]
        dattns = [mm(dmix, proj[l, 1, :, lanes], NT) for dmix, lanes in zip(dmixes, heads)]
        dvalues = [mm(attn[l, h], dmixes[h], TN) for h in range(HEADS)]
        dscores = [
            (dattn.astype(BF16).astype(F32) * attn_slope[l, h]).astype(BF16)
            for h, dattn in enumerate(dattns)
        ]
        dqueries = [mm(dscore, proj[l, 3, :, lanes]) for dscore, lanes in zip(dscores, heads)]
        dkeys = [mm(dscore, proj[l, 2, :, lanes], TN) for dscore, lanes in zip(dscores, heads)]
        for part, grads in ((1, dvalues), (2, dqueries), (3, dkeys)):
            for lanes, piece in zip(heads, grads):
                piece = piece.astype(BF16).astype(F32)
                dproj[part, :, lanes] = (piece * slope[l, part, :, lanes]).astype(BF16)
        value = normed[l]
        rounded = value.astype(BF16)
        dnormed = jnp.zeros((TOK, D), F32)
        for part in range(4):
            dpre = dproj[part]
            dnormed += mm(dpre, win_ref[l, :, part * D : (part + 1) * D], NT)
        for part in range(4):
            put(part, mm(rounded, dproj[part], TN).astype(BF16))
        dnormed = dnormed.astype(BF16).astype(F32)
        leave(*moves[1 - l], "start")
        stream[...] = grad + norm_back(dnormed, value, normed_scale[l])

    grad = stream[...]
    for pair in range(N_COL // 2):
        top = grad[:128, pair * 128 : (pair + 1) * 128]
        bottom = grad[128:, pair * 128 : (pair + 1) * 128]
        grad_ref[2 * pair] = jnp.concatenate([top[:, :COLS], bottom[:, :COLS]], axis=1).astype(BF16)
        grad_ref[2 * pair + 1] = jnp.concatenate([top[:, COLS:], bottom[:, COLS:]], axis=1).astype(BF16)
    hot_row = jnp.concatenate([index_ref[col, 0:1, :], index_ref[col, 1:2, :]], axis=1) - SLOTS
    pick = jnp.where(lax.broadcasted_iota(I32, (HOT, TOK), 0) == hot_row, 1.0, 0.0).astype(BF16)
    hot_part = mm(pick, grad.astype(BF16)).astype(BF16)
    for l in range(LAYERS):
        first, second = (x, y) if l == 0 else (y, z)
        for a in range(4):
            for b in range(4):
                chunk = 4 * a + b
                place = 4 * ((a - first) & 3) + ((b - second) & 3)
                pay[l, place, 160:CHUNK, :] = hot_part[chunk * 16 : (chunk + 1) * 16, :]
    for move in moves[2:]:
        leave(*move, "start")
    for move in moves:
        leave(*move, "wait")


def run_stack(index, emb, weight_in, weight_out, segment, cotangent):
    piece = jax.ShapeDtypeStruct((4, CHUNK, D), BF16)
    return pl.pallas_call(
        stack_kernel,
        out_shape=(
            jax.ShapeDtypeStruct((TOK, D), BF16),
            jax.ShapeDtypeStruct((N_COL, 128, 128), BF16),
        )
        + (piece,) * 8,
        in_specs=vmem(6),
        out_specs=tuple(vmem(2)) + (HBM,) * 8,
        scratch_shapes=[
            pltpu.VMEM((TOK, D), F32),
            pltpu.VMEM((LAYERS, TOK, D), F32),
            pltpu.VMEM((LAYERS, TOK, 1), F32),
            pltpu.VMEM((LAYERS, 4, TOK, D), BF16),
            pltpu.VMEM((LAYERS, 4, TOK, D), F32),
            pltpu.VMEM((LAYERS, HEADS, TOK, TOK), BF16),
            pltpu.VMEM((LAYERS, HEADS, TOK, TOK), F32),
            pltpu.VMEM((LAYERS, TOK, D), F32),
            pltpu.VMEM((LAYERS, TOK, 1), F32),
            pltpu.VMEM((LAYERS, TOK, D), BF16),
            pltpu.VMEM((4, TOK, D), BF16),
            pltpu.VMEM((LAYERS, 16, CHUNK, D), BF16),
            pltpu.SemaphoreType.DMA((4, 4)),
        ],
        compiler_params=params(36),
        cost_estimate=cost(16),
        name="layers",
    )(index, emb, segment, cotangent, weight_in, weight_out)


def device_pairs(move):
    pairs = []
    for z in range(4):
        for y in range(4):
            for x in range(4):
                for core in range(2):
                    tz, ty, tx, tcore = move(z, y, x, core)
                    pairs.append(
                        (((z * 4 + y) * 4 + x) * 2 + core, ((tz * 4 + ty) * 4 + tx) * 2 + tcore)
                    )
    return pairs


BOTH = ("seq", "col")


def to_core(value):
    return lax.ppermute(value, BOTH, device_pairs(lambda z, y, x, c: (z, y, x, 1 - c)))


def along(value, stage, k):
    def move(z, y, x, c):
        place = [x, y, z]
        axis = (stage + c) % 3
        place[axis] = (place[axis] + k) % 4
        return (place[2], place[1], place[0], c)

    return lax.ppermute(value, BOTH, device_pairs(move))


def add_all(*terms):
    terms = [t.astype(F32) for t in terms]
    while len(terms) > 1:
        terms = [a + b for a, b in zip(terms[::2], terms[1::2])]
    return terms[0].astype(BF16)


def sum_everywhere(keep, send, grad_emb, gather_columns, send_back, exchange, scatter):
    order = (2, 1, 3, 0)
    got = {k: to_core(send[k]) for k in order}
    chip = {k: add_all(keep[k], got[k]) for k in order}
    came = {k: along(chip[k], 0, k) for k in (2, 1, 3)}
    line = add_all(chip[0], came[2], came[1], came[3])
    line, grad_emb = lax.optimization_barrier((line, grad_emb))
    came = {k: along(line[k], 1, k) for k in (2, 1, 3)}
    plane = add_all(line[0], came[2], came[1], came[3])
    outgoing = send_back(gather_columns(grad_emb))
    came = {k: along(plane, 2, k) for k in (2, 1, 3)}
    total = add_all(plane, came[2], came[1], came[3])
    row = jnp.stack([total] + [along(total, 1, -k) for k in (1, 2, 3)])
    incoming = exchange(outgoing)
    mine = {k: along(row, 0, -k) for k in (2, 1, 3)}
    mine[0] = row
    other = {0: to_core(row)}
    table_grad = scatter(incoming)
    grads = finish([row, other[0]], [(0, True), (0, False)])
    pieces = lax.optimization_barrier((mine[1], mine[2], mine[3], table_grad, grads))
    mine[1], mine[2], mine[3], table_grad, grads = pieces
    other.update({k: to_core(mine[k]) for k in (1, 2, 3)})
    grads = finish([mine[k] for k in (1, 2, 3)], [(k, True) for k in (1, 2, 3)], grads)
    hot_grad = hot_sums([mine[k] for k in range(4)])
    grads = finish([other[k] for k in (1, 2, 3)], [(k, False) for k in (1, 2, 3)], grads)
    return grads[0], grads[1], hot_grad, table_grad


def finish_kernel(pieces, start, *refs):
    sources, refs = refs[: len(pieces)], refs[len(pieces) :]
    win_ref, wout_ref, stage_in, stage_out, sems = refs if start else refs[2:]
    (x, y, z), core = places()
    copies = []
    for i, (a, own) in enumerate(pieces):
        layer = core if own else 1 - core
        first = jnp.where(layer == 0, x, y)
        second = jnp.where(layer == 0, y, z)
        for b in range(4):
            chunk = 4 * ((a + first) & 3) + ((b + second) & 3)
            step = 4 * i + b
            for part in range(4):
                stage_in[step, :, part * D : (part + 1) * D] = sources[i][
                    b, part * 32 : (part + 1) * 32, :
                ].astype(F32)
            stage_out[step] = sources[i][b, 128:160, :].astype(F32)
            rows = pl.ds(pl.multiple_of(chunk * 32, 32), 32)
            here = [
                pltpu.make_async_copy(stage_in.at[step], win_ref.at[layer, rows], sems.at[step, 0]),
                pltpu.make_async_copy(stage_out.at[step], wout_ref.at[layer, rows], sems.at[step, 1]),
            ]
            for copy in here:
                copy.start()
            copies += here
    for copy in copies:
        copy.wait()


def finish(sources, pieces, partial=()):
    steps = 4 * len(pieces)
    return pl.pallas_call(
        functools.partial(finish_kernel, pieces, not partial),
        out_shape=(
            jax.ShapeDtypeStruct((LAYERS, D, 4 * D), F32),
            jax.ShapeDtypeStruct((LAYERS, D, D), F32),
        ),
        in_specs=vmem(len(pieces)) + [ANY] * len(partial),
        out_specs=(ANY, ANY),
        scratch_shapes=[
            pltpu.VMEM((steps, 32, 4 * D), F32),
            pltpu.VMEM((steps, 32, D), F32),
            pltpu.SemaphoreType.DMA((steps, 2)),
        ],
        input_output_aliases={len(pieces): 0, len(pieces) + 1: 1} if partial else {},
        compiler_params=params(6 + 3 * len(pieces)),
        cost_estimate=cost(0.5 + 0.6 * len(pieces)),
        name="widen_sums",
    )(*sources, *partial)


def hot_kernel(*refs):
    sources, hot_ref, rows = refs[:4], refs[4], refs[5]
    (x, y, z), core = places()
    col = lax.axis_index("col")
    first = jnp.where(core == 0, x, y)
    second = jnp.where(core == 0, y, z)
    for a in range(4):
        for b in range(4):
            chunk = 4 * ((a + first) & 3) + ((b + second) & 3)
            rows[pl.ds(pl.multiple_of(chunk * 16, 16), 16), :] = sources[a][b]
    pick = jnp.where(
        lax.broadcasted_iota(I32, (COLS, D), 1) == lax.broadcasted_iota(I32, (COLS, D), 0) + col * COLS,
        1.0,
        0.0,
    ).astype(BF16)
    hot_ref[...] = mm(pick, rows[...], NT)


def hot_sums(mine):
    return pl.pallas_call(
        hot_kernel,
        out_shape=jax.ShapeDtypeStruct((COLS, HOT), F32),
        in_specs=vmem(4),
        out_specs=vmem(1)[0],
        scratch_shapes=[pltpu.VMEM((HOT, D), BF16)],
        compiler_params=params(8),
        cost_estimate=cost(1),
        name="hot_sums",
    )(*[value[:, 160:CHUNK] for value in mine]).T


def on_device(
    item_table, hot_table, weight_in, weight_out, row_owner, item_row, hot_flag, hot_row, segment, cotangent
):
    line = (1, SEQ_TOK)
    requests, index = make_slots(
        row_owner.reshape(line), item_row.reshape(line), hot_flag.reshape(line), hot_row.reshape(line)
    )
    received = lax.all_to_all(requests, "seq", split_axis=0, concat_axis=0, tiled=True)
    picked = pick_rows(received, jnp.pad(item_table.astype(F32), ((0, 8), (0, 0))))
    returned = lax.all_to_all(picked, "seq", split_axis=0, concat_axis=0, tiled=True)
    placed = place_rows(index, returned, hot_table)
    emb = lax.all_to_all(placed, "col", split_axis=0, concat_axis=0, tiled=True)
    outs = run_stack(index, emb, weight_in, weight_out, segment, cotangent)
    encoded, grad_emb, keep, send = outs[0], outs[1], outs[2:6], outs[6:10]

    def gather_columns(grad_emb):
        return lax.all_to_all(grad_emb, "col", split_axis=0, concat_axis=0, tiled=True)

    def send_back(columns):
        return return_rows(index, columns)

    def exchange(outgoing):
        return lax.all_to_all(outgoing, "seq", split_axis=0, concat_axis=0, tiled=True)

    def scatter(incoming):
        return scatter_rows(received, incoming)

    grad_in, grad_out, hot_grad, table_grad = sum_everywhere(
        keep, send, grad_emb, gather_columns, send_back, exchange, scatter
    )
    return (encoded, table_grad, hot_grad, grad_in, grad_out)


def solution(mesh):
    in_specs = (
        P("seq", "col"),
        P(None, "col"),
        P(),
        P(),
        P("seq", None),
        P("seq"),
        P("seq"),
        P("seq"),
        P(("seq", "col"), None),
        P(("seq", "col"), None),
    )
    out_specs = (P(("seq", "col"), None), P("seq", "col"), P(None, "col"), P(), P())
    return jax.shard_map(
        on_device, mesh=mesh, in_specs=in_specs, out_specs=out_specs, check_vma=False
    )
```

```python
import functools

import jax
import jax.numpy as jnp
from jax import lax
from jax.experimental import pallas as pl
from jax.experimental.pallas import tpu as pltpu
from jax.sharding import PartitionSpec as P

F32 = jnp.float32
BF16 = jnp.bfloat16
I32 = jnp.int32

D = 512
HEADS = 4
HEAD_DIM = 128
LAYERS = 2
TOK = 256
N_SEQ = 16
N_COL = 8
SEQ_TOK = TOK * N_COL
CAP = 256
SLOTS = N_SEQ * CAP
ITEMS_DEV = 4096
HOT = 256
COLS = 64
CHUNK = 176
MIB = 1024 * 1024

NT = (((1,), (1,)), ((), ()))
TN = (((0,), (0,)), ((), ()))


def params(mib):
    return pltpu.CompilerParams(vmem_limit_bytes=mib * MIB)


def cost(microseconds):
    return pl.CostEstimate(
        flops=int(microseconds * 1.1e9), bytes_accessed=int(microseconds * 3.6e6), transcendentals=0
    )


def vmem(count):
    return [pl.BlockSpec(memory_space=pltpu.VMEM)] * count


SMEM = pl.BlockSpec(memory_space=pltpu.SMEM)
ANY = pl.BlockSpec(memory_space=pl.ANY)
HBM = pl.BlockSpec(memory_space=pltpu.HBM)


def mm(a, b, dims=None):
    if dims is None:
        return jnp.dot(a, b, preferred_element_type=F32)
    return lax.dot_general(a, b, dims, preferred_element_type=F32)


def slot_kernel(owner_ref, item_ref, flag_ref, hot_ref, request_ref, index_ref):
    owner = owner_ref[...]
    regular = flag_ref[...] == 0
    owners = lax.broadcasted_iota(I32, (N_SEQ, SEQ_TOK), 0)
    member = jnp.where((owners == owner) & regular, 1.0, 0.0)
    member_b = member.astype(BF16)
    upper = jnp.where(
        lax.broadcasted_iota(I32, (TOK, TOK), 0) <= lax.broadcasted_iota(I32, (TOK, TOK), 1), 1.0, 0.0
    ).astype(BF16)
    carry = jnp.zeros((N_SEQ, 1), F32)
    requests = jnp.zeros((3 * N_SEQ, CAP), F32)
    item = item_ref[...]
    high = (item >> 6).astype(F32)
    low = (item & 63).astype(F32)
    for block in range(N_COL):
        span = slice(block * TOK, (block + 1) * TOK)
        here = member[:, span]
        count = mm(member_b[:, span], upper) + carry
        carry = count[:, TOK - 1 : TOK]
        slot = jnp.sum((count - 1.0) * here, axis=0, keepdims=True).astype(I32)
        place = jnp.where(
            regular[:, span], owner[:, span] * CAP + slot, SLOTS + hot_ref[:, span]
        )
        index_ref[block, 0:1, :] = place[:, :128]
        index_ref[block, 1:2, :] = place[:, 128:]
        slots = lax.broadcasted_iota(I32, (CAP, TOK), 0)
        pick = jnp.where(slots == slot, 1.0, 0.0).astype(BF16)
        parts = jnp.concatenate([here * high[:, span], here * low[:, span], here], axis=0)
        requests += mm(parts.astype(BF16), pick, NT)
    rows = requests[:N_SEQ] * 64.0 + requests[N_SEQ : 2 * N_SEQ]
    rows = jnp.where(requests[2 * N_SEQ :] > 0.5, rows, float(ITEMS_DEV))
    rows = rows.astype(I32)
    request_ref[:, 0, :] = rows[:, :128]
    request_ref[:, 1, :] = rows[:, 128:]


def make_slots(owner, item, flag, hot):
    return pl.pallas_call(
        slot_kernel,
        out_shape=(
            jax.ShapeDtypeStruct((N_SEQ, 2, 128), I32),
            jax.ShapeDtypeStruct((N_COL, 2, 128), I32),
        ),
        in_specs=vmem(4),
        out_specs=tuple(vmem(2)),
        compiler_params=params(60),
        cost_estimate=cost(2.5),
        name="slots",
    )(owner, item, flag, hot)


def widen(packed):
    wide = packed.astype(F32)
    return wide[:, :COLS], wide[:, COLS:]


def narrow(rows):
    return jnp.concatenate([rows[:128], rows[128:]], axis=1).astype(BF16)


def each_row(count, body, unroll=64):
    def step(i, carry):
        for u in range(unroll):
            body(i * unroll + u)
        return carry

    lax.fori_loop(0, count // unroll, step, 0)


GROUP = 32


def pick_kernel(request_ref, table_ref, out_ref, rows):
    def group(i, carry):
        start = i * GROUP

        @pl.when(request_ref[start] < ITEMS_DEV)
        def asked():
            for u in range(GROUP):
                rows[pl.ds(start + u, 1), :] = table_ref[pl.ds(request_ref[start + u], 1), :]

        return carry

    lax.fori_loop(0, SLOTS // GROUP, group, 0)
    for requester in range(N_SEQ):
        out_ref[requester] = narrow(rows[requester * CAP : (requester + 1) * CAP, :])


def pick_rows(requests, table):
    return pl.pallas_call(
        pick_kernel,
        out_shape=jax.ShapeDtypeStruct((N_SEQ, 128, 128), BF16),
        in_specs=[SMEM] + vmem(1),
        out_specs=vmem(1)[0],
        scratch_shapes=[pltpu.VMEM((SLOTS, COLS), F32)],
        compiler_params=params(16),
        cost_estimate=cost(7),
        name="pick_rows",
    )(requests.reshape(SLOTS), table)


def place_kernel(index_ref, returned_ref, hot_ref, out_ref, source, rows):
    for owner in range(N_SEQ):
        first, second = widen(returned_ref[owner])
        source[owner * CAP : owner * CAP + 128, :] = first
        source[owner * CAP + 128 : (owner + 1) * CAP, :] = second
    source[SLOTS : SLOTS + HOT, :] = hot_ref[...].astype(F32).T

    def one(token):
        rows[pl.ds(token, 1), :] = source[pl.ds(index_ref[token], 1), :]

    each_row(SEQ_TOK, one)
    for block in range(N_COL):
        out_ref[block] = narrow(rows[block * TOK : (block + 1) * TOK, :])


def place_rows(index, returned, hot_table):
    return pl.pallas_call(
        place_kernel,
        out_shape=jax.ShapeDtypeStruct((N_COL, 128, 128), BF16),
        in_specs=[SMEM] + vmem(2),
        out_specs=vmem(1)[0],
        scratch_shapes=[pltpu.VMEM((SLOTS + HOT, COLS), F32), pltpu.VMEM((SEQ_TOK, COLS), F32)],
        compiler_params=params(16),
        cost_estimate=cost(4),
        name="place_rows",
    )(index.reshape(SEQ_TOK), returned, hot_table.T)


def return_kernel(index_ref, grad_ref, out_ref, rows, target):
    target[...] = jnp.zeros_like(target)
    for block in range(N_COL):
        first, second = widen(grad_ref[block])
        rows[block * TOK : block * TOK + 128, :] = first
        rows[block * TOK + 128 : (block + 1) * TOK, :] = second

    def one(token):
        target[pl.ds(index_ref[token], 1), :] = rows[pl.ds(token, 1), :]

    each_row(SEQ_TOK, one)
    for owner in range(N_SEQ):
        out_ref[owner] = narrow(target[owner * CAP : (owner + 1) * CAP, :])


def return_rows(index, grads):
    return pl.pallas_call(
        return_kernel,
        out_shape=jax.ShapeDtypeStruct((N_SEQ, 128, 128), BF16),
        in_specs=[SMEM] + vmem(1),
        out_specs=vmem(1)[0],
        scratch_shapes=[
            pltpu.VMEM((SEQ_TOK, COLS), F32),
            pltpu.VMEM((SLOTS + HOT, COLS), F32),
        ],
        compiler_params=params(16),
        cost_estimate=cost(4),
        name="return_rows",
    )(index.reshape(SEQ_TOK), grads)


def scatter_kernel(request_ref, incoming_ref, out_ref, rows, *totals):
    for total in totals:
        total[...] = jnp.zeros_like(total)
    for requester in range(N_SEQ):
        first, second = widen(incoming_ref[requester])
        rows[requester * CAP : requester * CAP + 128, :] = first
        rows[requester * CAP + 128 : (requester + 1) * CAP, :] = second
    part = SLOTS // len(totals)

    def group(i, carry):
        starts = [t * part + i * 8 for t in range(len(totals))]
        held = [request_ref[start] < ITEMS_DEV for start in starts]

        @pl.when(functools.reduce(jnp.logical_or, held))
        def some():
            for u in range(8):
                for start, total in zip(starts, totals):
                    slot = start + u
                    total[pl.ds(request_ref[slot], 1), :] += rows[pl.ds(slot, 1), :]

        return carry

    lax.fori_loop(0, part // 8, group, 0)
    for block in range(ITEMS_DEV // 128):
        span = slice(block * 128, (block + 1) * 128)
        value = totals[0][span, :]
        for total in totals[1:]:
            value = value + total[span, :]
        out_ref[:, span] = value.T


def scatter_rows(requests, incoming):
    return pl.pallas_call(
        scatter_kernel,
        out_shape=jax.ShapeDtypeStruct((COLS, ITEMS_DEV), F32),
        in_specs=[SMEM] + vmem(1),
        out_specs=vmem(1)[0],
        scratch_shapes=[pltpu.VMEM((SLOTS, COLS), F32)]
        + [pltpu.VMEM((ITEMS_DEV + 8, COLS), F32)] * 4,
        compiler_params=params(24),
        cost_estimate=cost(11),
        name="scatter_rows",
    )(requests.reshape(SLOTS), incoming).T


def norm(value):
    center = value - jnp.mean(value, axis=-1, keepdims=True)
    scale = lax.rsqrt(jnp.mean(center * center, axis=-1, keepdims=True) + 1e-05)
    return center * scale, scale


def norm_back(grad, normed, scale):
    shift = jnp.mean(grad, axis=-1, keepdims=True)
    tilt = jnp.mean(grad * normed, axis=-1, keepdims=True)
    return scale * (grad - shift - normed * tilt)


def silu_parts(value):
    gate = jax.nn.sigmoid(value)
    return value * gate, gate * (1.0 + value * (1.0 - gate))


def places():
    seq, col = lax.axis_index("seq"), lax.axis_index("col")
    return (col >> 1, seq & 3, seq >> 2), col & 1


def stack_kernel(
    index_ref, emb_ref, segment_ref, cot_ref, win_ref, wout_ref,
    enc_ref, grad_ref, *refs
):
    outs, refs = refs[:8], refs[8:]
    stream, normed, normed_scale, proj, slope, attn, attn_slope, mixed, mixed_scale, gated, dproj, pay, sems = refs
    keep, send = outs[:4], outs[4:]
    (x, y, z), core = places()

    def leave(l, span, sem, act):
        def each(targets):
            for a in range(4):
                copy = pltpu.make_async_copy(
                    pay.at[l, 4 * a : 4 * a + 4, span], targets[a].at[:, span], sems.at[sem, a]
                )
                getattr(copy, act)()

        pl.when(core == l)(lambda: each(keep))
        pl.when(core != l)(lambda: each(send))

    moves = tuple((l, span, i) for i, (l, span) in enumerate(
        ((1, slice(0, 160)), (0, slice(0, 160)), (1, slice(160, CHUNK)), (0, slice(160, CHUNK)))
    ))
    col = lax.axis_index("col")

    segment = jnp.broadcast_to(segment_ref[...].astype(F32), (TOK, TOK))
    row = lax.broadcasted_iota(I32, (TOK, TOK), 0)
    column = lax.broadcasted_iota(I32, (TOK, TOK), 1)
    allowed = (segment == segment.T) & (column <= row)

    for pair in range(N_COL // 2):
        a0, a1 = widen(emb_ref[2 * pair])
        b0, b1 = widen(emb_ref[2 * pair + 1])
        lanes = slice(pair * 128, (pair + 1) * 128)
        stream[:128, lanes] = jnp.concatenate([a0, b0], axis=1)
        stream[128:, lanes] = jnp.concatenate([a1, b1], axis=1)

    def lanes_of(head):
        return slice(head * HEAD_DIM, (head + 1) * HEAD_DIM)

    scaling = HEAD_DIM ** (-0.5)
    for l in range(LAYERS):
        value, scale = norm(stream[...])
        normed[l] = value
        normed_scale[l] = scale
        rounded = value.astype(BF16)
        for part in (2, 3, 1, 0):
            pre = mm(rounded, win_ref[l, :, part * D : (part + 1) * D])
            out, tilt = silu_parts(pre)
            proj[l, part] = out.astype(BF16)
            slope[l, part] = tilt
        scores = [mm(proj[l, 2, :, lanes_of(h)], proj[l, 3, :, lanes_of(h)], NT) for h in range(HEADS)]
        for head in range(HEADS):
            lanes = lanes_of(head)
            out, tilt = silu_parts(scores[head] * scaling)
            weight = jnp.where(allowed, out, 0.0).astype(BF16)
            attn[l, head] = weight
            attn_slope[l, head] = jnp.where(allowed, tilt * scaling, 0.0)
            mixed[l, :, lanes] = mm(weight, proj[l, 1, :, lanes])
        value, scale = norm(mixed[l])
        mixed[l] = value
        mixed_scale[l] = scale
        product = (value * proj[l, 0].astype(F32)).astype(BF16)
        gated[l] = product
        stream[...] += mm(product, wout_ref[l])
    enc_ref[...] = stream[...].astype(BF16)

    stream[...] = cot_ref[...].astype(F32)
    for l in reversed(range(LAYERS)):
        first, second = (x, y) if l == 0 else (y, z)

        def put(part, value):
            for a in range(4):
                for b in range(4):
                    chunk = 4 * a + b
                    place = 4 * ((a - first) & 3) + ((b - second) & 3)
                    pay[l, place, part * 32 : (part + 1) * 32, :] = value[chunk * 32 : (chunk + 1) * 32, :]

        grad = stream[...]
        grad_b = grad.astype(BF16)
        put(4, mm(gated[l], grad_b, TN).astype(BF16))
        dgated = mm(grad_b, wout_ref[l], NT).astype(BF16).astype(F32)
        hat = mixed[l]
        dproj[0] = ((dgated * hat).astype(BF16).astype(F32) * slope[l, 0]).astype(BF16)
        dmixed = norm_back(dgated * proj[l, 0].astype(F32), hat, mixed_scale[l]).astype(BF16)
        heads = [lanes_of(h) for h in range(HEADS)]
        dmixes = [dmixed[:, lanes] for lanes in heads]
        dattns = [mm(dmix, proj[l, 1, :, lanes], NT) for dmix, lanes in zip(dmixes, heads)]
        dvalues = [mm(attn[l, h], dmixes[h], TN) for h in range(HEADS)]
        dscores = [
            (dattn.astype(BF16).astype(F32) * attn_slope[l, h]).astype(BF16)
            for h, dattn in enumerate(dattns)
        ]
        dqueries = [mm(dscore, proj[l, 3, :, lanes]) for dscore, lanes in zip(dscores, heads)]
        dkeys = [mm(dscore, proj[l, 2, :, lanes], TN) for dscore, lanes in zip(dscores, heads)]
        for part, grads in ((1, dvalues), (2, dqueries), (3, dkeys)):
            for lanes, piece in zip(heads, grads):
                piece = piece.astype(BF16).astype(F32)
                dproj[part, :, lanes] = (piece * slope[l, part, :, lanes]).astype(BF16)
        value = normed[l]
        rounded = value.astype(BF16)
        dnormed = jnp.zeros((TOK, D), F32)
        for part in range(4):
            dpre = dproj[part]
            dnormed += mm(dpre, win_ref[l, :, part * D : (part + 1) * D], NT)
        for part in range(4):
            put(part, mm(rounded, dproj[part], TN).astype(BF16))
        dnormed = dnormed.astype(BF16).astype(F32)
        leave(*moves[1 - l], "start")
        stream[...] = grad + norm_back(dnormed, value, normed_scale[l])

    grad = stream[...]
    for pair in range(N_COL // 2):
        top = grad[:128, pair * 128 : (pair + 1) * 128]
        bottom = grad[128:, pair * 128 : (pair + 1) * 128]
        grad_ref[2 * pair] = jnp.concatenate([top[:, :COLS], bottom[:, :COLS]], axis=1).astype(BF16)
        grad_ref[2 * pair + 1] = jnp.concatenate([top[:, COLS:], bottom[:, COLS:]], axis=1).astype(BF16)
    hot_row = jnp.concatenate([index_ref[col, 0:1, :], index_ref[col, 1:2, :]], axis=1) - SLOTS
    pick = jnp.where(lax.broadcasted_iota(I32, (HOT, TOK), 0) == hot_row, 1.0, 0.0).astype(BF16)
    hot_part = mm(pick, grad.astype(BF16)).astype(BF16)
    for l in range(LAYERS):
        first, second = (x, y) if l == 0 else (y, z)
        for a in range(4):
            for b in range(4):
                chunk = 4 * a + b
                place = 4 * ((a - first) & 3) + ((b - second) & 3)
                pay[l, place, 160:CHUNK, :] = hot_part[chunk * 16 : (chunk + 1) * 16, :]
    for move in moves[2:]:
        leave(*move, "start")
    for move in moves:
        leave(*move, "wait")


def run_stack(index, emb, weight_in, weight_out, segment, cotangent):
    piece = jax.ShapeDtypeStruct((4, CHUNK, D), BF16)
    return pl.pallas_call(
        stack_kernel,
        out_shape=(
            jax.ShapeDtypeStruct((TOK, D), BF16),
            jax.ShapeDtypeStruct((N_COL, 128, 128), BF16),
        )
        + (piece,) * 8,
        in_specs=vmem(6),
        out_specs=tuple(vmem(2)) + (ANY,) * 8,
        scratch_shapes=[
            pltpu.VMEM((TOK, D), F32),
            pltpu.VMEM((LAYERS, TOK, D), F32),
            pltpu.VMEM((LAYERS, TOK, 1), F32),
            pltpu.VMEM((LAYERS, 4, TOK, D), BF16),
            pltpu.VMEM((LAYERS, 4, TOK, D), F32),
            pltpu.VMEM((LAYERS, HEADS, TOK, TOK), BF16),
            pltpu.VMEM((LAYERS, HEADS, TOK, TOK), F32),
            pltpu.VMEM((LAYERS, TOK, D), F32),
            pltpu.VMEM((LAYERS, TOK, 1), F32),
            pltpu.VMEM((LAYERS, TOK, D), BF16),
            pltpu.VMEM((4, TOK, D), BF16),
            pltpu.VMEM((LAYERS, 16, CHUNK, D), BF16),
            pltpu.SemaphoreType.DMA((4, 4)),
        ],
        compiler_params=params(36),
        cost_estimate=cost(16),
        name="layers",
    )(index, emb, segment, cotangent, weight_in, weight_out)


def device_pairs(move):
    pairs = []
    for z in range(4):
        for y in range(4):
            for x in range(4):
                for core in range(2):
                    tz, ty, tx, tcore = move(z, y, x, core)
                    pairs.append(
                        (((z * 4 + y) * 4 + x) * 2 + core, ((tz * 4 + ty) * 4 + tx) * 2 + tcore)
                    )
    return pairs


BOTH = ("seq", "col")


def to_core(value):
    return lax.ppermute(value, BOTH, device_pairs(lambda z, y, x, c: (z, y, x, 1 - c)))


def along(value, stage, k):
    def move(z, y, x, c):
        place = [x, y, z]
        axis = (stage + c) % 3
        place[axis] = (place[axis] + k) % 4
        return (place[2], place[1], place[0], c)

    return lax.ppermute(value, BOTH, device_pairs(move))


def add_all(*terms):
    terms = [t.astype(F32) for t in terms]
    while len(terms) > 1:
        terms = [a + b for a, b in zip(terms[::2], terms[1::2])]
    return terms[0].astype(BF16)


def sum_everywhere(keep, send, grad_emb, gather_columns, send_back, exchange, scatter):
    order = (2, 1, 3, 0)
    got = {k: to_core(send[k]) for k in order}
    chip = {k: add_all(keep[k], got[k]) for k in order}
    came = {k: along(chip[k], 0, k) for k in (1, 3, 2)}
    line = add_all(chip[0], came[2], came[1], came[3])
    line, grad_emb = lax.optimization_barrier((line, grad_emb))
    came = {k: along(line[k], 1, k) for k in (1, 3, 2)}
    plane = add_all(line[0], came[2], came[1], came[3])
    outgoing = send_back(gather_columns(grad_emb))
    came = {k: along(plane, 2, k) for k in (1, 3, 2)}
    total = add_all(plane, came[2], came[1], came[3])
    row = jnp.stack([total] + [along(total, 1, -k) for k in (1, 2, 3)])
    incoming = exchange(outgoing)
    mine = {k: along(row, 0, -k) for k in (1, 3, 2)}
    mine[0] = row
    other = {0: to_core(row)}
    table_grad = scatter(incoming)
    grads = finish([row, other[0]], [(0, True), (0, False)])
    pieces = lax.optimization_barrier((mine[1], mine[2], mine[3], table_grad, grads))
    mine[1], mine[2], mine[3], table_grad, grads = pieces
    other.update({k: to_core(mine[k]) for k in (1, 2, 3)})
    grads = finish([mine[k] for k in (1, 2, 3)], [(k, True) for k in (1, 2, 3)], grads)
    hot_grad = hot_sums([mine[k] for k in range(4)])
    grads = finish([other[k] for k in (1, 2, 3)], [(k, False) for k in (1, 2, 3)], grads)
    return grads[0], grads[1], hot_grad, table_grad


def finish_kernel(pieces, start, *refs):
    sources, refs = refs[: len(pieces)], refs[len(pieces) :]
    win_ref, wout_ref, stage_in, stage_out, sems = refs if start else refs[2:]
    (x, y, z), core = places()
    copies = []
    for i, (a, own) in enumerate(pieces):
        layer = core if own else 1 - core
        first = jnp.where(layer == 0, x, y)
        second = jnp.where(layer == 0, y, z)
        for b in range(4):
            chunk = 4 * ((a + first) & 3) + ((b + second) & 3)
            step = 4 * i + b
            for part in range(4):
                stage_in[step, :, part * D : (part + 1) * D] = sources[i][
                    b, part * 32 : (part + 1) * 32, :
                ].astype(F32)
            stage_out[step] = sources[i][b, 128:160, :].astype(F32)
            rows = pl.ds(pl.multiple_of(chunk * 32, 32), 32)
            here = [
                pltpu.make_async_copy(stage_in.at[step], win_ref.at[layer, rows], sems.at[step, 0]),
                pltpu.make_async_copy(stage_out.at[step], wout_ref.at[layer, rows], sems.at[step, 1]),
            ]
            for copy in here:
                copy.start()
            copies += here
    for copy in copies:
        copy.wait()


def finish(sources, pieces, partial=()):
    steps = 4 * len(pieces)
    return pl.pallas_call(
        functools.partial(finish_kernel, pieces, not partial),
        out_shape=(
            jax.ShapeDtypeStruct((LAYERS, D, 4 * D), F32),
            jax.ShapeDtypeStruct((LAYERS, D, D), F32),
        ),
        in_specs=vmem(len(pieces)) + [ANY] * len(partial),
        out_specs=(ANY, ANY),
        scratch_shapes=[
            pltpu.VMEM((steps, 32, 4 * D), F32),
            pltpu.VMEM((steps, 32, D), F32),
            pltpu.SemaphoreType.DMA((steps, 2)),
        ],
        input_output_aliases={len(pieces): 0, len(pieces) + 1: 1} if partial else {},
        compiler_params=params(6 + 3 * len(pieces)),
        cost_estimate=cost(0.5 + 0.6 * len(pieces)),
        name="widen_sums",
    )(*sources, *partial)


def hot_kernel(*refs):
    sources, hot_ref, rows = refs[:4], refs[4], refs[5]
    (x, y, z), core = places()
    col = lax.axis_index("col")
    first = jnp.where(core == 0, x, y)
    second = jnp.where(core == 0, y, z)
    for a in range(4):
        for b in range(4):
            chunk = 4 * ((a + first) & 3) + ((b + second) & 3)
            rows[pl.ds(pl.multiple_of(chunk * 16, 16), 16), :] = sources[a][b]
    pick = jnp.where(
        lax.broadcasted_iota(I32, (COLS, D), 1) == lax.broadcasted_iota(I32, (COLS, D), 0) + col * COLS,
        1.0,
        0.0,
    ).astype(BF16)
    hot_ref[...] = mm(pick, rows[...], NT)


def hot_sums(mine):
    return pl.pallas_call(
        hot_kernel,
        out_shape=jax.ShapeDtypeStruct((COLS, HOT), F32),
        in_specs=vmem(4),
        out_specs=vmem(1)[0],
        scratch_shapes=[pltpu.VMEM((HOT, D), BF16)],
        compiler_params=params(8),
        cost_estimate=cost(1),
        name="hot_sums",
    )(*[value[:, 160:CHUNK] for value in mine]).T


def on_device(
    item_table, hot_table, weight_in, weight_out, row_owner, item_row, hot_flag, hot_row, segment, cotangent
):
    line = (1, SEQ_TOK)
    requests, index = make_slots(
        row_owner.reshape(line), item_row.reshape(line), hot_flag.reshape(line), hot_row.reshape(line)
    )
    received = lax.all_to_all(requests, "seq", split_axis=0, concat_axis=0, tiled=True)
    picked = pick_rows(received, jnp.pad(item_table.astype(F32), ((0, 8), (0, 0))))
    returned = lax.all_to_all(picked, "seq", split_axis=0, concat_axis=0, tiled=True)
    placed = place_rows(index, returned, hot_table)
    emb = lax.all_to_all(placed, "col", split_axis=0, concat_axis=0, tiled=True)
    outs = run_stack(index, emb, weight_in, weight_out, segment, cotangent)
    encoded, grad_emb, keep, send = outs[0], outs[1], outs[2:6], outs[6:10]

    def gather_columns(grad_emb):
        return lax.all_to_all(grad_emb, "col", split_axis=0, concat_axis=0, tiled=True)

    def send_back(columns):
        return return_rows(index, columns)

    def exchange(outgoing):
        return lax.all_to_all(outgoing, "seq", split_axis=0, concat_axis=0, tiled=True)

    def scatter(incoming):
        return scatter_rows(received, incoming)

    grad_in, grad_out, hot_grad, table_grad = sum_everywhere(
        keep, send, grad_emb, gather_columns, send_back, exchange, scatter
    )
    return (encoded, table_grad, hot_grad, grad_in, grad_out)


def solution(mesh):
    in_specs = (
        P("seq", "col"),
        P(None, "col"),
        P(),
        P(),
        P("seq", None),
        P("seq"),
        P("seq"),
        P("seq"),
        P(("seq", "col"), None),
        P(("seq", "col"), None),
    )
    out_specs = (P(("seq", "col"), None), P("seq", "col"), P(None, "col"), P(), P())
    return jax.shard_map(
        on_device, mesh=mesh, in_specs=in_specs, out_specs=out_specs, check_vma=False
    )
```

```python
import functools

import jax
import jax.numpy as jnp
from jax import lax
from jax.experimental import pallas as pl
from jax.experimental.pallas import tpu as pltpu
from jax.sharding import PartitionSpec as P

F32 = jnp.float32
BF16 = jnp.bfloat16
I32 = jnp.int32

D = 512
HEADS = 4
HEAD_DIM = 128
LAYERS = 2
TOK = 256
N_SEQ = 16
N_COL = 8
SEQ_TOK = TOK * N_COL
CAP = 256
SLOTS = N_SEQ * CAP
ITEMS_DEV = 4096
HOT = 256
COLS = 64
CHUNK = 176
MIB = 1024 * 1024

NT = (((1,), (1,)), ((), ()))
TN = (((0,), (0,)), ((), ()))


def params(mib):
    return pltpu.CompilerParams(vmem_limit_bytes=mib * MIB)


def cost(microseconds):
    return pl.CostEstimate(
        flops=int(microseconds * 1.1e9), bytes_accessed=int(microseconds * 3.6e6), transcendentals=0
    )


def vmem(count):
    return [pl.BlockSpec(memory_space=pltpu.VMEM)] * count


SMEM = pl.BlockSpec(memory_space=pltpu.SMEM)
ANY = pl.BlockSpec(memory_space=pl.ANY)
HBM = pl.BlockSpec(memory_space=pltpu.HBM)


def mm(a, b, dims=None):
    if dims is None:
        return jnp.dot(a, b, preferred_element_type=F32)
    return lax.dot_general(a, b, dims, preferred_element_type=F32)


def slot_kernel(owner_ref, item_ref, flag_ref, hot_ref, request_ref, index_ref):
    owner = owner_ref[...]
    regular = flag_ref[...] == 0
    owners = lax.broadcasted_iota(I32, (N_SEQ, SEQ_TOK), 0)
    member = jnp.where((owners == owner) & regular, 1.0, 0.0)
    member_b = member.astype(BF16)
    upper = jnp.where(
        lax.broadcasted_iota(I32, (TOK, TOK), 0) <= lax.broadcasted_iota(I32, (TOK, TOK), 1), 1.0, 0.0
    ).astype(BF16)
    item = item_ref[...]
    parts = jnp.concatenate(
        [member * (item >> 6).astype(F32), member * (item & 63).astype(F32), member], axis=0
    ).astype(BF16)
    spans = [slice(block * TOK, (block + 1) * TOK) for block in range(N_COL)]
    counts = [mm(member_b[:, span], upper) for span in spans]
    carry = jnp.zeros((N_SEQ, 1), F32)
    slots = lax.broadcasted_iota(I32, (CAP, TOK), 0)
    picks = []
    for block, span in enumerate(spans):
        count = counts[block] + carry
        carry = carry + counts[block][:, TOK - 1 : TOK]
        slot = jnp.sum((count - 1.0) * member[:, span], axis=0, keepdims=True).astype(I32)
        place = jnp.where(
            regular[:, span], owner[:, span] * CAP + slot, SLOTS + hot_ref[:, span]
        )
        index_ref[block, 0:1, :] = place[:, :128]
        index_ref[block, 1:2, :] = place[:, 128:]
        picks.append(jnp.where(slots == slot, 1.0, 0.0).astype(BF16))
    requests = mm(parts, jnp.concatenate(picks, axis=1), NT)
    rows = requests[:N_SEQ] * 64.0 + requests[N_SEQ : 2 * N_SEQ]
    rows = jnp.where(requests[2 * N_SEQ :] > 0.5, rows, float(ITEMS_DEV))
    rows = rows.astype(I32)
    request_ref[:, 0, :] = rows[:, :128]
    request_ref[:, 1, :] = rows[:, 128:]


def make_slots(owner, item, flag, hot):
    return pl.pallas_call(
        slot_kernel,
        out_shape=(
            jax.ShapeDtypeStruct((N_SEQ, 2, 128), I32),
            jax.ShapeDtypeStruct((N_COL, 2, 128), I32),
        ),
        in_specs=vmem(4),
        out_specs=tuple(vmem(2)),
        compiler_params=params(60),
        cost_estimate=cost(2.5),
        name="slots",
    )(owner, item, flag, hot)


def widen(packed):
    wide = packed.astype(F32)
    return wide[:, :COLS], wide[:, COLS:]


def narrow(rows):
    return jnp.concatenate([rows[:128], rows[128:]], axis=1).astype(BF16)


def each_row(count, body, unroll=64):
    def step(i, carry):
        for u in range(unroll):
            body(i * unroll + u)
        return carry

    lax.fori_loop(0, count // unroll, step, 0)


GROUP = 32


def pick_kernel(request_ref, table_ref, out_ref, rows):
    def group(i, carry):
        start = i * GROUP

        @pl.when(request_ref[start] < ITEMS_DEV)
        def asked():
            for u in range(GROUP):
                rows[pl.ds(start + u, 1), :] = table_ref[pl.ds(request_ref[start + u], 1), :]

        return carry

    lax.fori_loop(0, SLOTS // GROUP, group, 0)
    for requester in range(N_SEQ):
        out_ref[requester] = narrow(rows[requester * CAP : (requester + 1) * CAP, :])


def pick_rows(requests, table):
    return pl.pallas_call(
        pick_kernel,
        out_shape=jax.ShapeDtypeStruct((N_SEQ, 128, 128), BF16),
        in_specs=[SMEM] + vmem(1),
        out_specs=vmem(1)[0],
        scratch_shapes=[pltpu.VMEM((SLOTS, COLS), F32)],
        compiler_params=params(16),
        cost_estimate=cost(7),
        name="pick_rows",
    )(requests.reshape(SLOTS), table)


def place_kernel(index_ref, returned_ref, hot_ref, out_ref, source, rows):
    for owner in range(N_SEQ):
        first, second = widen(returned_ref[owner])
        source[owner * CAP : owner * CAP + 128, :] = first
        source[owner * CAP + 128 : (owner + 1) * CAP, :] = second
    source[SLOTS : SLOTS + HOT, :] = hot_ref[...].astype(F32).T

    def one(token):
        rows[pl.ds(token, 1), :] = source[pl.ds(index_ref[token], 1), :]

    each_row(SEQ_TOK, one)
    for block in range(N_COL):
        out_ref[block] = narrow(rows[block * TOK : (block + 1) * TOK, :])


def place_rows(index, returned, hot_table):
    return pl.pallas_call(
        place_kernel,
        out_shape=jax.ShapeDtypeStruct((N_COL, 128, 128), BF16),
        in_specs=[SMEM] + vmem(2),
        out_specs=vmem(1)[0],
        scratch_shapes=[pltpu.VMEM((SLOTS + HOT, COLS), F32), pltpu.VMEM((SEQ_TOK, COLS), F32)],
        compiler_params=params(16),
        cost_estimate=cost(4),
        name="place_rows",
    )(index.reshape(SEQ_TOK), returned, hot_table.T)


def return_kernel(index_ref, grad_ref, out_ref, rows, target):
    target[...] = jnp.zeros_like(target)
    for block in range(N_COL):
        first, second = widen(grad_ref[block])
        rows[block * TOK : block * TOK + 128, :] = first
        rows[block * TOK + 128 : (block + 1) * TOK, :] = second

    def one(token):
        target[pl.ds(index_ref[token], 1), :] = rows[pl.ds(token, 1), :]

    each_row(SEQ_TOK, one)
    for owner in range(N_SEQ):
        out_ref[owner] = narrow(target[owner * CAP : (owner + 1) * CAP, :])


def return_rows(index, grads):
    return pl.pallas_call(
        return_kernel,
        out_shape=jax.ShapeDtypeStruct((N_SEQ, 128, 128), BF16),
        in_specs=[SMEM] + vmem(1),
        out_specs=vmem(1)[0],
        scratch_shapes=[
            pltpu.VMEM((SEQ_TOK, COLS), F32),
            pltpu.VMEM((SLOTS + HOT, COLS), F32),
        ],
        compiler_params=params(16),
        cost_estimate=cost(4),
        name="return_rows",
    )(index.reshape(SEQ_TOK), grads)


def scatter_kernel(request_ref, incoming_ref, out_ref, rows, *totals):
    for total in totals:
        total[...] = jnp.zeros_like(total)
    for requester in range(N_SEQ):
        first, second = widen(incoming_ref[requester])
        rows[requester * CAP : requester * CAP + 128, :] = first
        rows[requester * CAP + 128 : (requester + 1) * CAP, :] = second
    part = SLOTS // len(totals)

    def group(i, carry):
        starts = [t * part + i * 8 for t in range(len(totals))]
        held = [request_ref[start] < ITEMS_DEV for start in starts]

        @pl.when(functools.reduce(jnp.logical_or, held))
        def some():
            for u in range(8):
                for start, total in zip(starts, totals):
                    slot = start + u
                    total[pl.ds(request_ref[slot], 1), :] += rows[pl.ds(slot, 1), :]

        return carry

    lax.fori_loop(0, part // 8, group, 0)
    for block in range(ITEMS_DEV // 128):
        span = slice(block * 128, (block + 1) * 128)
        value = totals[0][span, :]
        for total in totals[1:]:
            value = value + total[span, :]
        out_ref[:, span] = value.T


def scatter_rows(requests, incoming):
    return pl.pallas_call(
        scatter_kernel,
        out_shape=jax.ShapeDtypeStruct((COLS, ITEMS_DEV), F32),
        in_specs=[SMEM] + vmem(1),
        out_specs=vmem(1)[0],
        scratch_shapes=[pltpu.VMEM((SLOTS, COLS), F32)]
        + [pltpu.VMEM((ITEMS_DEV + 8, COLS), F32)] * 4,
        compiler_params=params(24),
        cost_estimate=cost(11),
        name="scatter_rows",
    )(requests.reshape(SLOTS), incoming).T


def norm(value):
    center = value - jnp.mean(value, axis=-1, keepdims=True)
    scale = lax.rsqrt(jnp.mean(center * center, axis=-1, keepdims=True) + 1e-05)
    return center * scale, scale


def norm_back(grad, normed, scale):
    shift = jnp.mean(grad, axis=-1, keepdims=True)
    tilt = jnp.mean(grad * normed, axis=-1, keepdims=True)
    return scale * (grad - shift - normed * tilt)


def silu_parts(value):
    gate = jax.nn.sigmoid(value)
    return value * gate, gate * (1.0 + value * (1.0 - gate))


def places():
    seq, col = lax.axis_index("seq"), lax.axis_index("col")
    return (col >> 1, seq & 3, seq >> 2), col & 1


def stack_kernel(
    index_ref, emb_ref, segment_ref, cot_ref, win_ref, wout_ref,
    enc_ref, grad_ref, *refs
):
    outs, refs = refs[:8], refs[8:]
    stream, normed, normed_scale, proj, slope, attn, attn_slope, mixed, mixed_scale, gated, dproj, pay, sems = refs
    keep, send = outs[:4], outs[4:]
    (x, y, z), core = places()

    def leave(l, span, sem, act):
        def each(targets):
            for a in range(4):
                copy = pltpu.make_async_copy(
                    pay.at[l, 4 * a : 4 * a + 4, span], targets[a].at[:, span], sems.at[sem, a]
                )
                getattr(copy, act)()

        pl.when(core == l)(lambda: each(keep))
        pl.when(core != l)(lambda: each(send))

    moves = tuple((l, span, i) for i, (l, span) in enumerate(
        ((1, slice(0, 160)), (0, slice(0, 160)), (1, slice(160, CHUNK)), (0, slice(160, CHUNK)))
    ))
    col = lax.axis_index("col")

    segment = jnp.broadcast_to(segment_ref[...].astype(F32), (TOK, TOK))
    row = lax.broadcasted_iota(I32, (TOK, TOK), 0)
    column = lax.broadcasted_iota(I32, (TOK, TOK), 1)
    allowed = (segment == segment.T) & (column <= row)

    for pair in range(N_COL // 2):
        a0, a1 = widen(emb_ref[2 * pair])
        b0, b1 = widen(emb_ref[2 * pair + 1])
        lanes = slice(pair * 128, (pair + 1) * 128)
        stream[:128, lanes] = jnp.concatenate([a0, b0], axis=1)
        stream[128:, lanes] = jnp.concatenate([a1, b1], axis=1)

    def lanes_of(head):
        return slice(head * HEAD_DIM, (head + 1) * HEAD_DIM)

    scaling = HEAD_DIM ** (-0.5)
    for l in range(LAYERS):
        value, scale = norm(stream[...])
        normed[l] = value
        normed_scale[l] = scale
        rounded = value.astype(BF16)
        for part in (2, 3, 1, 0):
            pre = mm(rounded, win_ref[l, :, part * D : (part + 1) * D])
            out, tilt = silu_parts(pre)
            proj[l, part] = out.astype(BF16)
            slope[l, part] = tilt
        scores = [mm(proj[l, 2, :, lanes_of(h)], proj[l, 3, :, lanes_of(h)], NT) for h in range(HEADS)]
        for head in range(HEADS):
            lanes = lanes_of(head)
            out, tilt = silu_parts(scores[head] * scaling)
            weight = jnp.where(allowed, out, 0.0).astype(BF16)
            attn[l, head] = weight
            attn_slope[l, head] = jnp.where(allowed, tilt * scaling, 0.0)
            mixed[l, :, lanes] = mm(weight, proj[l, 1, :, lanes])
        value, scale = norm(mixed[l])
        mixed[l] = value
        mixed_scale[l] = scale
        product = (value * proj[l, 0].astype(F32)).astype(BF16)
        gated[l] = product
        stream[...] += mm(product, wout_ref[l])
    enc_ref[...] = stream[...].astype(BF16)

    stream[...] = cot_ref[...].astype(F32)
    for l in reversed(range(LAYERS)):
        first, second = (x, y) if l == 0 else (y, z)

        def put(part, value):
            for a in range(4):
                for b in range(4):
                    chunk = 4 * a + b
                    place = 4 * ((a - first) & 3) + ((b - second) & 3)
                    pay[l, place, part * 32 : (part + 1) * 32, :] = value[chunk * 32 : (chunk + 1) * 32, :]

        grad = stream[...]
        grad_b = grad.astype(BF16)
        dgated = mm(grad_b, wout_ref[l], NT).astype(BF16).astype(F32)
        hat = mixed[l]
        dproj[0] = ((dgated * hat).astype(BF16).astype(F32) * slope[l, 0]).astype(BF16)
        dmixed = norm_back(dgated * proj[l, 0].astype(F32), hat, mixed_scale[l]).astype(BF16)
        heads = [lanes_of(h) for h in range(HEADS)]
        dmixes = [dmixed[:, lanes] for lanes in heads]
        dattns = [mm(dmix, proj[l, 1, :, lanes], NT) for dmix, lanes in zip(dmixes, heads)]
        dvalues = [mm(attn[l, h], dmixes[h], TN) for h in range(HEADS)]
        dscores = [
            (dattn.astype(BF16).astype(F32) * attn_slope[l, h]).astype(BF16)
            for h, dattn in enumerate(dattns)
        ]
        dqueries = [mm(dscore, proj[l, 3, :, lanes]) for dscore, lanes in zip(dscores, heads)]
        dkeys = [mm(dscore, proj[l, 2, :, lanes], TN) for dscore, lanes in zip(dscores, heads)]
        for part, grads in ((1, dvalues), (2, dqueries), (3, dkeys)):
            for lanes, piece in zip(heads, grads):
                piece = piece.astype(BF16).astype(F32)
                dproj[part, :, lanes] = (piece * slope[l, part, :, lanes]).astype(BF16)
        value = normed[l]
        rounded = value.astype(BF16)
        dnormed = jnp.zeros((TOK, D), F32)
        for part in range(4):
            dpre = dproj[part]
            dnormed += mm(dpre, win_ref[l, :, part * D : (part + 1) * D], NT)
        put(4, mm(gated[l], grad_b, TN).astype(BF16))
        for part in range(4):
            put(part, mm(rounded, dproj[part], TN).astype(BF16))
        dnormed = dnormed.astype(BF16).astype(F32)
        leave(*moves[1 - l], "start")
        stream[...] = grad + norm_back(dnormed, value, normed_scale[l])

    grad = stream[...]
    for pair in range(N_COL // 2):
        top = grad[:128, pair * 128 : (pair + 1) * 128]
        bottom = grad[128:, pair * 128 : (pair + 1) * 128]
        grad_ref[2 * pair] = jnp.concatenate([top[:, :COLS], bottom[:, :COLS]], axis=1).astype(BF16)
        grad_ref[2 * pair + 1] = jnp.concatenate([top[:, COLS:], bottom[:, COLS:]], axis=1).astype(BF16)
    hot_row = jnp.concatenate([index_ref[col, 0:1, :], index_ref[col, 1:2, :]], axis=1) - SLOTS
    pick = jnp.where(lax.broadcasted_iota(I32, (HOT, TOK), 0) == hot_row, 1.0, 0.0).astype(BF16)
    hot_part = mm(pick, grad.astype(BF16)).astype(BF16)
    for l in range(LAYERS):
        first, second = (x, y) if l == 0 else (y, z)
        for a in range(4):
            for b in range(4):
                chunk = 4 * a + b
                place = 4 * ((a - first) & 3) + ((b - second) & 3)
                pay[l, place, 160:CHUNK, :] = hot_part[chunk * 16 : (chunk + 1) * 16, :]
    for move in moves[2:]:
        leave(*move, "start")
    for move in moves:
        leave(*move, "wait")


def run_stack(index, emb, weight_in, weight_out, segment, cotangent):
    piece = jax.ShapeDtypeStruct((4, CHUNK, D), BF16)
    return pl.pallas_call(
        stack_kernel,
        out_shape=(
            jax.ShapeDtypeStruct((TOK, D), BF16),
            jax.ShapeDtypeStruct((N_COL, 128, 128), BF16),
        )
        + (piece,) * 8,
        in_specs=vmem(6),
        out_specs=tuple(vmem(2)) + (ANY,) * 8,
        scratch_shapes=[
            pltpu.VMEM((TOK, D), F32),
            pltpu.VMEM((LAYERS, TOK, D), F32),
            pltpu.VMEM((LAYERS, TOK, 1), F32),
            pltpu.VMEM((LAYERS, 4, TOK, D), BF16),
            pltpu.VMEM((LAYERS, 4, TOK, D), F32),
            pltpu.VMEM((LAYERS, HEADS, TOK, TOK), BF16),
            pltpu.VMEM((LAYERS, HEADS, TOK, TOK), F32),
            pltpu.VMEM((LAYERS, TOK, D), F32),
            pltpu.VMEM((LAYERS, TOK, 1), F32),
            pltpu.VMEM((LAYERS, TOK, D), BF16),
            pltpu.VMEM((4, TOK, D), BF16),
            pltpu.VMEM((LAYERS, 16, CHUNK, D), BF16),
            pltpu.SemaphoreType.DMA((4, 4)),
        ],
        compiler_params=params(36),
        cost_estimate=cost(16),
        name="layers",
    )(index, emb, segment, cotangent, weight_in, weight_out)


def device_pairs(move):
    pairs = []
    for z in range(4):
        for y in range(4):
            for x in range(4):
                for core in range(2):
                    tz, ty, tx, tcore = move(z, y, x, core)
                    pairs.append(
                        (((z * 4 + y) * 4 + x) * 2 + core, ((tz * 4 + ty) * 4 + tx) * 2 + tcore)
                    )
    return pairs


BOTH = ("seq", "col")


def to_core(value):
    return lax.ppermute(value, BOTH, device_pairs(lambda z, y, x, c: (z, y, x, 1 - c)))


def along(value, stage, k):
    def move(z, y, x, c):
        place = [x, y, z]
        axis = (stage + c) % 3
        place[axis] = (place[axis] + k) % 4
        return (place[2], place[1], place[0], c)

    return lax.ppermute(value, BOTH, device_pairs(move))


def add_all(*terms):
    terms = [t.astype(F32) for t in terms]
    while len(terms) > 1:
        terms = [a + b for a, b in zip(terms[::2], terms[1::2])]
    return terms[0].astype(BF16)


def sum_everywhere(keep, send, grad_emb, gather_columns, send_back, exchange, scatter):
    order = (2, 1, 3, 0)
    got = {k: to_core(send[k]) for k in order}
    chip = {k: add_all(keep[k], got[k]) for k in order}
    came = {k: along(chip[k], 0, k) for k in (1, 3, 2)}
    line = add_all(chip[0], came[2], came[1], came[3])
    line, grad_emb = lax.optimization_barrier((line, grad_emb))
    came = {k: along(line[k], 1, k) for k in (1, 3, 2)}
    plane = add_all(line[0], came[2], came[1], came[3])
    outgoing = send_back(gather_columns(grad_emb))
    came = {k: along(plane, 2, k) for k in (1, 3, 2)}
    total = add_all(plane, came[2], came[1], came[3])
    row = jnp.stack([total] + [along(total, 1, -k) for k in (1, 2, 3)])
    incoming = exchange(outgoing)
    mine = {k: along(row, 0, -k) for k in (1, 3, 2)}
    mine[0] = row
    other = {0: to_core(row)}
    table_grad = scatter(incoming)
    grads = finish([row, other[0]], [(0, True), (0, False)])
    pieces = lax.optimization_barrier((mine[1], mine[2], mine[3], table_grad, grads))
    mine[1], mine[2], mine[3], table_grad, grads = pieces
    other.update({k: to_core(mine[k]) for k in (1, 2, 3)})
    grads = finish([mine[k] for k in (1, 2, 3)], [(k, True) for k in (1, 2, 3)], grads)
    hot_grad = hot_sums([mine[k] for k in range(4)])
    grads = finish([other[k] for k in (1, 2, 3)], [(k, False) for k in (1, 2, 3)], grads)
    return grads[0], grads[1], hot_grad, table_grad


def finish_kernel(pieces, start, *refs):
    sources, refs = refs[: len(pieces)], refs[len(pieces) :]
    win_ref, wout_ref, stage_in, stage_out, sems = refs if start else refs[2:]
    (x, y, z), core = places()
    copies = []
    for i, (a, own) in enumerate(pieces):
        layer = core if own else 1 - core
        first = jnp.where(layer == 0, x, y)
        second = jnp.where(layer == 0, y, z)
        for b in range(4):
            chunk = 4 * ((a + first) & 3) + ((b + second) & 3)
            step = 4 * i + b
            for part in range(4):
                stage_in[step, :, part * D : (part + 1) * D] = sources[i][
                    b, part * 32 : (part + 1) * 32, :
                ].astype(F32)
            stage_out[step] = sources[i][b, 128:160, :].astype(F32)
            rows = pl.ds(pl.multiple_of(chunk * 32, 32), 32)
            here = [
                pltpu.make_async_copy(stage_in.at[step], win_ref.at[layer, rows], sems.at[step, 0]),
                pltpu.make_async_copy(stage_out.at[step], wout_ref.at[layer, rows], sems.at[step, 1]),
            ]
            for copy in here:
                copy.start()
            copies += here
    for copy in copies:
        copy.wait()


def finish(sources, pieces, partial=()):
    steps = 4 * len(pieces)
    return pl.pallas_call(
        functools.partial(finish_kernel, pieces, not partial),
        out_shape=(
            jax.ShapeDtypeStruct((LAYERS, D, 4 * D), F32),
            jax.ShapeDtypeStruct((LAYERS, D, D), F32),
        ),
        in_specs=vmem(len(pieces)) + [ANY] * len(partial),
        out_specs=(ANY, ANY),
        scratch_shapes=[
            pltpu.VMEM((steps, 32, 4 * D), F32),
            pltpu.VMEM((steps, 32, D), F32),
            pltpu.SemaphoreType.DMA((steps, 2)),
        ],
        input_output_aliases={len(pieces): 0, len(pieces) + 1: 1} if partial else {},
        compiler_params=params(6 + 3 * len(pieces)),
        cost_estimate=cost(0.5 + 0.6 * len(pieces)),
        name="widen_sums",
    )(*sources, *partial)


def hot_kernel(*refs):
    sources, hot_ref, rows = refs[:4], refs[4], refs[5]
    (x, y, z), core = places()
    col = lax.axis_index("col")
    first = jnp.where(core == 0, x, y)
    second = jnp.where(core == 0, y, z)
    for a in range(4):
        for b in range(4):
            chunk = 4 * ((a + first) & 3) + ((b + second) & 3)
            rows[pl.ds(pl.multiple_of(chunk * 16, 16), 16), :] = sources[a][b]
    pick = jnp.where(
        lax.broadcasted_iota(I32, (COLS, D), 1) == lax.broadcasted_iota(I32, (COLS, D), 0) + col * COLS,
        1.0,
        0.0,
    ).astype(BF16)
    hot_ref[...] = mm(pick, rows[...], NT)


def hot_sums(mine):
    return pl.pallas_call(
        hot_kernel,
        out_shape=jax.ShapeDtypeStruct((COLS, HOT), F32),
        in_specs=vmem(4),
        out_specs=vmem(1)[0],
        scratch_shapes=[pltpu.VMEM((HOT, D), BF16)],
        compiler_params=params(8),
        cost_estimate=cost(1),
        name="hot_sums",
    )(*[value[:, 160:CHUNK] for value in mine]).T


def on_device(
    item_table, hot_table, weight_in, weight_out, row_owner, item_row, hot_flag, hot_row, segment, cotangent
):
    line = (1, SEQ_TOK)
    requests, index = make_slots(
        row_owner.reshape(line), item_row.reshape(line), hot_flag.reshape(line), hot_row.reshape(line)
    )
    received = lax.all_to_all(requests, "seq", split_axis=0, concat_axis=0, tiled=True)
    picked = pick_rows(received, jnp.pad(item_table.astype(F32), ((0, 8), (0, 0))))
    returned = lax.all_to_all(picked, "seq", split_axis=0, concat_axis=0, tiled=True)
    placed = place_rows(index, returned, hot_table)
    emb = lax.all_to_all(placed, "col", split_axis=0, concat_axis=0, tiled=True)
    outs = run_stack(index, emb, weight_in, weight_out, segment, cotangent)
    encoded, grad_emb, keep, send = outs[0], outs[1], outs[2:6], outs[6:10]

    def gather_columns(grad_emb):
        return lax.all_to_all(grad_emb, "col", split_axis=0, concat_axis=0, tiled=True)

    def send_back(columns):
        return return_rows(index, columns)

    def exchange(outgoing):
        return lax.all_to_all(outgoing, "seq", split_axis=0, concat_axis=0, tiled=True)

    def scatter(incoming):
        return scatter_rows(received, incoming)

    grad_in, grad_out, hot_grad, table_grad = sum_everywhere(
        keep, send, grad_emb, gather_columns, send_back, exchange, scatter
    )
    return (encoded, table_grad, hot_grad, grad_in, grad_out)


def solution(mesh):
    in_specs = (
        P("seq", "col"),
        P(None, "col"),
        P(),
        P(),
        P("seq", None),
        P("seq"),
        P("seq"),
        P("seq"),
        P(("seq", "col"), None),
        P(("seq", "col"), None),
    )
    out_specs = (P(("seq", "col"), None), P("seq", "col"), P(None, "col"), P(), P())
    return jax.shard_map(
        on_device, mesh=mesh, in_specs=in_specs, out_specs=out_specs, check_vma=False
    )
```
